768 devices in a mesh: slab: 96 (over y, z), cut: 8 (over x, core).
Axes of the slice: x: 4, y: 8, z: 12, core: 2. Of those that a mesh axis runs over, the one named last changes fastest.
Arguments:
- conserved: float32 [5, 512, 98304], P(None, None, ('slab', 'cut')), may hold values from -2 to 21, as said below
- refinement: int32 [98304], P(('slab', 'cut')), may hold values from 0 to 2
- x_neighbour: int32 [768, 128], P(('slab', 'cut')), may hold values from 0 to 127, each once within a row
- coarse_element: int32 [96, 8, 4, 32], P('slab', 'cut'), may hold values from 0 to 127, as said below
- quadrant: int32 [96, 8, 4, 32], P('slab', 'cut'), may hold values from 0 to 3, as said below
- send_count: int32 [96, 8, 4], P('slab', 'cut'), may hold values from 8 to 32, as said below
- fine_element: int32 [96, 8, 4, 32], P('slab', 'cut'), may hold values from 0 to 127, as said below
- orientation: int32 [96, 8, 4, 32], P('slab', 'cut'), may hold values from 0 to 3
- receive_count: int32 [96, 8, 4], P('slab', 'cut'), may hold values from 8 to 32, as said below
Outputs:
- advanced: float32 [5, 512, 98304], P(None, None, ('slab', 'cut'))
- register: float32 [5, 512, 98304], P(None, None, ('slab', 'cut'))
The draws below stay inside these ranges and needn't reach their ends.
Inputs may be any that keep to these rules, and one draw needn't show every extreme that they name: `conserved`: density lies in 0.6 to 1.4 and pressure is positive at every node. `coarse_element`: slots j and j2 of one device and offset with j // 4 == j2 // 4 name the same element, and no element is named in two such groups of a device. `quadrant`: within each group of 4 slots (j // 4 equal) the sub-faces 0 to 3 appear once each; sub-face q covers half q // 2 along a and half q % 2 along c. `send_count`: for every offset some device sends 32 live links. `fine_element`: no element is named twice on one device. receive_count[s, t, o] equals send_count[(s - k_o) mod 96, t, o].
All inputs are finite; a program needn't handle non-finite values.
Results may differ from the reference program's by a relative error of at most 0.0003.
Values sent between devices are 32-bit elements; how exact they have to be, the bound alone decides.
A program may use at most 128 MiB of HBM per device.

```python
import math
import jax
import jax.numpy as jnp
import numpy as np
from jax import lax

NP = 8
NVAR = 5
NODES = 512
ELEM_DEV = 128
OFFS = 4
CAP = 32
ELEMS = 98304
N_SLAB = 96
N_CUT = 8


def offset_distance_drawn(offset_index):
    return (offset_index // 2 + 1) * (1 - 2 * (offset_index % 2))


def shuffled(subkey):
    return jax.random.permutation(subkey, ELEM_DEV)


def link_tables(key):
    devices = N_SLAB * N_CUT
    subkeys = jax.random.split(key, 6)
    counts = jax.random.randint(subkeys[0], (devices, OFFS), CAP // 4, CAP + 1)
    chosen = jax.random.randint(subkeys[1], (OFFS,), 0, devices)
    counts = jnp.where(jnp.arange(devices)[:, None] == chosen[None, :], CAP, counts)
    coarse_perm = jax.vmap(shuffled)(jax.random.split(subkeys[2], devices))
    slot_ids = jnp.arange(CAP)
    groups = jnp.arange(OFFS)[:, None] * (CAP // 4) + slot_ids[None, :] // 4
    coarse_element = coarse_perm[:, groups]
    group_turn = jax.random.randint(subkeys[3], (devices, OFFS, CAP // 4), 0, 4)
    quadrant = (slot_ids[None, None, :] % 4 + jnp.repeat(group_turn, 4, axis=2)) % 4
    fine_perm = jax.vmap(shuffled)(jax.random.split(subkeys[4], devices))
    fine_element = fine_perm[:, jnp.arange(OFFS * CAP).reshape(OFFS, CAP)]
    orientation = jax.random.randint(subkeys[5], (devices, OFFS, CAP), 0, 4)
    sent_count = counts.reshape(N_SLAB, N_CUT, OFFS)
    received = jnp.stack([jnp.roll(sent_count[:, :, offset_index], offset_distance_drawn(offset_index), axis=0) for offset_index in range(OFFS)], axis=2)
    link_shape = (N_SLAB, N_CUT, OFFS, CAP)
    return (coarse_element.reshape(link_shape).astype(jnp.int32), quadrant.reshape(link_shape).astype(jnp.int32), sent_count.astype(jnp.int32), fine_element.reshape(link_shape).astype(jnp.int32), orientation.reshape(link_shape).astype(jnp.int32), received.astype(jnp.int32))


def draw_coarse_element(key, part):
    return link_tables(key)[0]


def draw_quadrant(key, part):
    return link_tables(key)[1]


def draw_send_count(key, part):
    return link_tables(key)[2]


def draw_fine_element(key, part):
    return link_tables(key)[3]


def draw_orientation(key, part):
    return link_tables(key)[4]


def draw_receive_count(key, part):
    return link_tables(key)[5]


def draw_conserved(key, part):
    key = jax.random.fold_in(key, 3)
    devices = N_SLAB * N_CUT
    position = (jnp.arange(ELEMS) // ELEM_DEV).astype(jnp.float32) / max(devices - 1, 1)
    pressure_scale = 0.5 * jnp.exp(position * math.log(9.0))
    rough = jnp.clip(0.5 * jax.random.normal(key, (NVAR, NODES, ELEMS), jnp.float32), -1.0, 1.0)
    density = 1.0 + 0.4 * rough[0]
    pressure = pressure_scale * (1.0 + 0.4 * rough[1])
    sound_speed = jnp.sqrt(1.4 * pressure_scale)
    velocity = sound_speed * (0.3 * rough[2:5])
    momentum = density * velocity
    energy = pressure / 0.4 + 0.5 * density * jnp.sum(velocity * velocity, axis=0)
    return jnp.concatenate([density[None], momentum, energy[None]]).astype(jnp.float32)


def place_ends(array, key, least, high):
    shape = array.shape
    spot = [jax.random.randint(jax.random.fold_in(key, axis), (), 0, shape[axis]) for axis in range(len(shape))]
    array = array.at[tuple(spot)].set(least)
    longest = shape.index(max(shape))
    spot[longest] = (spot[longest] + 1) % shape[longest]
    return array.at[tuple(spot)].set(high)


def setup_inputs(seed: int = 0) -> dict:
    key_of = jax.random.split(jax.random.key(seed), 10)
    conserved = draw_conserved(jax.random.fold_in(key_of[9], 71), 0)
    refinement = place_ends(jax.random.randint(key_of[1], (ELEMS,), 0, 3), jax.random.fold_in(key_of[1], 1), 0, 2).astype(jnp.int32)
    x_neighbour = jax.vmap(lambda own: jax.random.permutation(own, ELEM_DEV))(jax.random.split(key_of[2], (N_SLAB * N_CUT))).reshape((N_SLAB * N_CUT, ELEM_DEV)).astype(jnp.int32)
    coarse_element = draw_coarse_element(jax.random.fold_in(key_of[9], 71), 0)
    quadrant = draw_quadrant(jax.random.fold_in(key_of[9], 71), 0)
    send_count = draw_send_count(jax.random.fold_in(key_of[9], 71), 0)
    fine_element = draw_fine_element(jax.random.fold_in(key_of[9], 71), 0)
    orientation = draw_orientation(jax.random.fold_in(key_of[9], 71), 0)
    receive_count = draw_receive_count(jax.random.fold_in(key_of[9], 71), 0)
    return {"conserved": conserved, "refinement": refinement, "x_neighbour": x_neighbour, "coarse_element": coarse_element, "quadrant": quadrant, "send_count": send_count, "fine_element": fine_element, "orientation": orientation, "receive_count": receive_count}


gamma_ratio = 1.4
courant = 0.005
section_a = (0.0, -567301805773.0 / 1357537059087.0)
section_b = (1432997174477.0 / 9575080441755.0, 5161836677717.0 / 13612068292357.0)

def legendre_rows(points, node_count):
    legendre = np.zeros((node_count, node_count))
    legendre[:, 0] = 1.0
    legendre[:, 1] = points
    for degree in range(2, node_count):
        legendre[:, degree] = ((2 * degree - 1) * points * legendre[:, degree - 1] - (degree - 1) * legendre[:, degree - 2]) / degree
    return legendre

def lobatto(node_count):
    poly_order = node_count - 1
    points = -np.cos(np.pi * np.arange(node_count) / poly_order)
    for newton_step in range(40):
        legendre = legendre_rows(points, node_count)
        points = points - (points * legendre[:, poly_order] - legendre[:, poly_order - 1]) / (node_count * legendre[:, poly_order])
    top_row = legendre_rows(points, node_count)[:, poly_order]
    weights = 2.0 / (poly_order * node_count * top_row * top_row)
    differ = np.zeros((node_count, node_count))
    for target in range(node_count):
        for source in range(node_count):
            if target != source:
                differ[target, source] = top_row[target] / (top_row[source] * (points[target] - points[source]))
    differ[0, 0] = -poly_order * node_count / 4.0
    differ[poly_order, poly_order] = poly_order * node_count / 4.0
    to_half = np.zeros((2, node_count, node_count))
    for half_side in range(2):
        targets = (points + 2 * half_side - 1) / 2.0
        for source in range(node_count):
            basis = np.ones(node_count)
            for other in range(node_count):
                if other != source:
                    basis = basis * (targets - points[other]) / (points[source] - points[other])
            to_half[half_side, :, source] = basis
    from_half = 0.5 * np.transpose(to_half, (0, 2, 1)) * weights[None, None, :] / weights[None, :, None]
    return (weights, differ, to_half, from_half)

def make_tables():
    return tuple((jnp.asarray(table, dtype=jnp.float32) for table in lobatto(NP)))

def level_metric(refinement):
    return jnp.where(refinement == 0, 1.0, jnp.where(refinement == 1, 2.0, 4.0)).astype(jnp.float32)

def offset_distance(offset_index):
    return (offset_index // 2 + 1) * (1 - 2 * (offset_index % 2))

def primitives(state):
    density = state[0]
    velocity = state[1:4] / density
    pressure = (gamma_ratio - 1.0) * (state[4] - 0.5 * lax.optimization_barrier(jnp.sum(state[1:4] * velocity, axis=0)))
    return (density, velocity, pressure)

def directional_flux(state, velocity, pressure, direction):
    normal_speed = velocity[direction]
    flux_rows = [state[1 + direction]]
    for column in range(3):
        carried = state[1 + column] * normal_speed
        flux_rows.append(carried + pressure if column == direction else carried)
    flux_rows.append(normal_speed * (state[4] + pressure))
    return jnp.stack(flux_rows)

def face_flux(state, direction):
    density, velocity, pressure = primitives(state)
    sound_speed = jnp.sqrt(gamma_ratio * pressure / density)
    return (directional_flux(state, velocity, pressure, direction), jnp.abs(velocity[direction]) + sound_speed)

def numerical_flux(left_state, right_state, direction):
    left_flux, left_speed = face_flux(left_state, direction)
    right_flux, right_speed = face_flux(right_state, direction)
    fastest = jnp.maximum(left_speed, right_speed)
    flux_star = 0.5 * (left_flux + right_flux) - 0.5 * fastest * (right_state - left_state)
    return (flux_star, left_flux, right_flux)

def wave_speed(state5, metric):
    density, velocity, pressure = primitives(state5)
    return metric * (jnp.sqrt(lax.optimization_barrier(jnp.sum(velocity * velocity, axis=0))) + jnp.sqrt(gamma_ratio * pressure / density))

def sub_face(values, quadrant, matrices):
    highest = lax.Precision.HIGHEST
    along_a = [jnp.einsum('ia,vac...->vic...', matrices[half_side], values, precision=highest) for half_side in range(2)]
    chosen = jnp.where(quadrant // 2 == 1, along_a[1], along_a[0])
    along_c = [jnp.einsum('jc,vic...->vij...', matrices[half_side], chosen, precision=highest) for half_side in range(2)]
    return jnp.where(quadrant % 2 == 1, along_c[1], along_c[0])

def rotate_turns(values, turns):
    options = [jnp.rot90(values, turn_count, axes=(1, 2)) for turn_count in range(4)]
    result = options[0]
    for turn_count in range(1, 4):
        result = jnp.where(turns == turn_count, options[turn_count], result)
    return result

def take_last(values, index):
    shaped = index.reshape((1,) * (values.ndim - index.ndim) + index.shape)
    return jnp.take_along_axis(values, shaped, axis=-1)

def local_rate(state5, metric, neighbour, below_top, above_bottom, coarse_face, fine_face, tables):
    weights, differ, to_half, from_half = tables
    highest = lax.Precision.HIGHEST
    far_node = NP - 1
    density, velocity, pressure = primitives(state5)
    fluxes = [directional_flux(state5, velocity, pressure, direction) for direction in range(3)]
    volume = jnp.einsum('ia,vabc...->vibc...', differ, fluxes[0], precision=highest)
    volume = volume + jnp.einsum('jb,vabc...->vajc...', differ, fluxes[1], precision=highest)
    volume = volume + jnp.einsum('kc,vabc...->vabk...', differ, fluxes[2], precision=highest)
    flux_star, left_flux, right_flux = numerical_flux(state5[:, far_node], take_last(state5[:, 0], neighbour), 0)
    x_plus = flux_star - left_flux
    x_minus = take_last(right_flux - flux_star, jnp.argsort(neighbour, axis=-1))
    flux_star, left_flux, right_flux = numerical_flux(state5[:, :, :, far_node], above_bottom, 2)
    z_plus = flux_star - left_flux
    flux_star, left_flux, right_flux = numerical_flux(below_top, state5[:, :, :, 0], 2)
    z_minus = right_flux - flux_star
    surface = jnp.zeros_like(state5)
    surface = surface.at[:, far_node].add(x_plus)
    surface = surface.at[:, 0].add(x_minus)
    surface = surface.at[:, :, far_node].add(coarse_face)
    surface = surface.at[:, :, 0].add(fine_face)
    surface = surface.at[:, :, :, far_node].add(z_plus)
    surface = surface.at[:, :, :, 0].add(z_minus)
    return -metric * (volume + surface / weights[0])

def reference(conserved, refinement, x_neighbour, coarse_element, quadrant, send_count, fine_element, orientation, receive_count):
    tables = make_tables()
    weights, differ, to_half, from_half = tables
    slabs = N_SLAB
    cuts = N_CUT
    per_device = ELEM_DEV
    links = OFFS * CAP
    far_node = NP - 1
    metric = level_metric(refinement).reshape(slabs, cuts, per_device)
    neighbour = x_neighbour.reshape(slabs, cuts, per_device)
    state_slabs = jnp.moveaxis(conserved.reshape(NVAR, NP, NP, NP, slabs, cuts, per_device), 4, 0)
    coarse_index = coarse_element.reshape(slabs, cuts, links)
    coarse_quadrant = quadrant.reshape(slabs, cuts, links)
    fine_index = fine_element.reshape(slabs, cuts, links)
    fine_turns = orientation.reshape(slabs, cuts, links)
    slot_ids = jnp.arange(CAP)
    coarse_live = (slot_ids < send_count[..., None]).reshape(slabs, cuts, links)
    fine_live = (slot_ids < receive_count[..., None]).reshape(slabs, cuts, links)

    def align_links(values, direction_sign):
        pieces = []
        for offset_index in range(OFFS):
            lower = offset_index * CAP
            pieces.append(jnp.roll(values[..., lower:lower + CAP], direction_sign * offset_distance(offset_index), axis=3))
        return jnp.concatenate(pieces, axis=-1)

    def gather_sum(values, index):
        segment_ids = (jnp.arange(slabs * cuts)[:, None] * per_device + index.reshape(slabs * cuts, links)).reshape(-1).astype(jnp.int32)
        flat_values = values.reshape(NVAR * NP * NP, slabs * cuts * links).T
        summed = jax.ops.segment_sum(flat_values, segment_ids, num_segments=slabs * cuts * per_device)
        return jnp.moveaxis(summed.T.reshape(NVAR, NP, NP, slabs, cuts, per_device), 3, 0)

    def mortar_terms(current):
        plus_face = jnp.moveaxis(current[:, :, :, far_node], 0, 3)
        minus_face = jnp.moveaxis(current[:, :, :, 0], 0, 3)
        coarse_trace = jnp.take_along_axis(plus_face, coarse_index[None, None, None], axis=5)
        mortar_coarse = sub_face(coarse_trace, coarse_quadrant, to_half)
        fine_trace = jnp.take_along_axis(minus_face, fine_index[None, None, None], axis=5)
        mortar_fine = align_links(rotate_turns(fine_trace, (4 - fine_turns) % 4), -1)
        flux_star, left_flux, right_flux = numerical_flux(mortar_coarse, mortar_fine, 1)
        coarse_values = jnp.where(coarse_live, sub_face(flux_star - left_flux, coarse_quadrant, from_half), 0.0)
        fine_values = jnp.where(fine_live, rotate_turns(align_links(right_flux - flux_star, 1), fine_turns), 0.0)
        return (gather_sum(coarse_values, coarse_index), gather_sum(fine_values, fine_index))

    def one_slab(pieces):
        piece, metric_piece, neighbour_piece, coarse_face, fine_face = pieces
        below_top = jnp.roll(piece[:, :, :, far_node], 1, axis=-2)
        above_bottom = jnp.roll(piece[:, :, :, 0], -1, axis=-2)
        return local_rate(piece, metric_piece, neighbour_piece, below_top, above_bottom, coarse_face, fine_face, tables)

    def operate(current):
        coarse_face, fine_face = mortar_terms(current)
        return lax.map(one_slab, (current, metric, neighbour, coarse_face, fine_face))

    def slab_speed(pieces):
        piece, metric_piece = pieces
        return jnp.max(wave_speed(piece, metric_piece))
    fastest = jnp.max(lax.map(slab_speed, (state_slabs, metric)))
    step_size = courant / fastest
    register = step_size * operate(state_slabs)
    sectioned = state_slabs + section_b[0] * register
    register = section_a[1] * register + step_size * operate(sectioned)
    advanced = sectioned + section_b[1] * register
    whole_shape = (NVAR, NP * NP * NP, slabs * cuts * per_device)
    return (jnp.moveaxis(advanced, 0, 4).reshape(whole_shape), jnp.moveaxis(register, 0, 4).reshape(whole_shape))
```

```python
import functools

import jax
import jax.numpy as jnp
import numpy as np
from jax import lax
from jax.experimental import pallas as pl
from jax.experimental.pallas import tpu as pltpu
from jax.sharding import PartitionSpec as P

NP = 8
NVAR = 5
FACE = NP * NP
LANES = 128
OFFS = 4
CAP = 32
MESH = pl.DeviceIdType.MESH

section_a = (0.0, -567301805773.0 / 1357537059087.0)
section_b = (1432997174477.0 / 9575080441755.0, 5161836677717.0 / 13612068292357.0)


def legendre_rows(points, node_count):
    legendre = np.zeros((node_count, node_count))
    legendre[:, 0] = 1.0
    legendre[:, 1] = points
    for degree in range(2, node_count):
        legendre[:, degree] = (
            (2 * degree - 1) * points * legendre[:, degree - 1]
            - (degree - 1) * legendre[:, degree - 2]
        ) / degree
    return legendre


def lobatto(node_count):
    poly_order = node_count - 1
    points = -np.cos(np.pi * np.arange(node_count) / poly_order)
    for newton_step in range(40):
        legendre = legendre_rows(points, node_count)
        points = points - (points * legendre[:, poly_order] - legendre[:, poly_order - 1]) / (
            node_count * legendre[:, poly_order]
        )
    top_row = legendre_rows(points, node_count)[:, poly_order]
    weights = 2.0 / (poly_order * node_count * top_row * top_row)
    differ = np.zeros((node_count, node_count))
    for target in range(node_count):
        for source in range(node_count):
            if target != source:
                differ[target, source] = top_row[target] / (
                    top_row[source] * (points[target] - points[source])
                )
    differ[0, 0] = -poly_order * node_count / 4.0
    differ[poly_order, poly_order] = poly_order * node_count / 4.0
    lower_half = np.zeros((node_count, node_count))
    targets = (points - 1) / 2.0
    for source in range(node_count):
        basis = np.ones(node_count)
        for other in range(node_count):
            if other != source:
                basis = basis * (targets - points[other]) / (points[source] - points[other])
        lower_half[:, source] = basis
    lower_back = 0.5 * np.transpose(lower_half) * weights[None, :] / weights[:, None]
    return (weights, differ, lower_half, lower_back)


WEIGHTS, DIFFER, HALF, BACK = lobatto(NP)
LIFT = float(1.0 / WEIGHTS[0])
EVEN = 0.5 * (DIFFER[:4, :4] + DIFFER[:4, :3:-1])
ODD = 0.5 * (DIFFER[:4, :4] - DIFFER[:4, :3:-1])


def combine(row, values):
    total = None
    for weight, value in zip(row, values):
        weight = float(np.float32(weight))
        if abs(weight) < 1e-12:
            continue
        term = value if weight == 1.0 else weight * value
        total = term if total is None else total + term
    return total


def derive(f):
    even = [f[j] + f[7 - j] for j in range(4)]
    odd = [f[j] - f[7 - j] for j in range(4)]
    out = [None] * 8
    for i in range(4):
        from_even = combine(EVEN[i], even)
        from_odd = combine(ODD[i], odd)
        out[i] = from_odd + from_even
        out[7 - i] = from_odd - from_even
    return out


def half_map(matrix, upper, f):
    f = [jnp.where(upper, f[7 - j], f[j]) for j in range(8)]
    g = [combine(matrix[i], f) for i in range(8)]
    return [jnp.where(upper, g[7 - i], g[i]) for i in range(8)]


def primitives(u):
    inverse = 1.0 / u[0]
    velocity = [u[1] * inverse, u[2] * inverse, u[3] * inverse]
    carried = u[1] * velocity[0] + u[2] * velocity[1] + u[3] * velocity[2]
    pressure = 0.4 * (u[4] - 0.5 * carried)
    return inverse, velocity, pressure


def flux_of(u, normal, pressure, direction):
    rows = [u[1 + direction]]
    for column in range(3):
        carried = u[1 + column] * normal
        rows.append(carried + pressure if column == direction else carried)
    rows.append(normal * (u[4] + pressure))
    return rows


def face_flux(u, direction):
    inverse, velocity, pressure = primitives(u)
    normal = velocity[direction]
    speed = jnp.abs(normal) + jnp.sqrt(1.4 * pressure * inverse)
    return flux_of(u, normal, pressure, direction), speed


def face_parts(left, right, direction):
    left_flux, left_speed = face_flux(left, direction)
    right_flux, right_speed = face_flux(right, direction)
    half_speed = 0.5 * jnp.maximum(left_speed, right_speed)
    mean = [0.5 * (r - l) for l, r in zip(left_flux, right_flux)]
    jump = [half_speed * (r - l) for l, r in zip(left, right)]
    return mean, jump


def lane_pick(x, index):
    return jnp.take_along_axis(x, index, axis=1, mode="promise_in_bounds")


def swap_blocks(x, lane):
    high = lane >= 64
    odd = (lane // 32) % 2 == 1
    y = list(x)
    for k in (0, 1):
        y[k] = jnp.where(high, pltpu.roll(x[k + 2], 64, 1), x[k])
        y[k + 2] = jnp.where(high, x[k + 2], pltpu.roll(x[k], 64, 1))
    z = list(y)
    for k in (0, 2):
        z[k] = jnp.where(odd, pltpu.roll(y[k + 1], 32, 1), y[k])
        z[k + 1] = jnp.where(odd, y[k + 1], pltpu.roll(y[k], 96, 1))
    return z


def offset_distance(offset_index):
    return (offset_index // 2 + 1) * (1 - 2 * (offset_index % 2))


def eight(row):
    return jnp.broadcast_to(row, (8, LANES))


def tile(i):
    return pl.ds(pl.multiple_of(i * 8, 8), 8)


def kernel(
    slabs, cuts, ys, zs,
    u_ref, ints_ref,
    adv_ref, reg_ref,
    prim, rate, sect,
    zsend, zrecv, csend, crecv, fsend, frecv,
    vsend, vrecv,
    own_coarse, own_fine, far_coarse, far_fine, work, packed,
    zs_sem, zr_sem, cs_sem, cr_sem, fs_sem, fr_sem, vs_sem, vr_sem,
):
    s = lax.axis_index("slab")
    t = lax.axis_index("cut")
    y = s // zs
    z = s % zs
    cut_peers = [(s, (t + d) % cuts) for d in range(1, cuts)]
    y_peers = [(((y + d) % ys) * zs + z, t) for d in range(1, ys)]
    z_peers = [(y * zs + (z + d) % zs, t) for d in range(1, zs)]
    ahead = [((s + offset_distance(o) + slabs) % slabs, t) for o in range(OFFS)]
    back = [((s - offset_distance(o) + slabs) % slabs, t) for o in range(OFFS)]

    barrier = pltpu.get_barrier_semaphore()
    greeted = cut_peers + y_peers + z_peers + ahead
    for peer in greeted:
        pl.semaphore_signal(barrier, inc=1, device_id=peer, device_id_type=MESH)

    lane = lax.broadcasted_iota(jnp.int32, (8, LANES), 1)
    sub = lax.broadcasted_iota(jnp.int32, (8, LANES), 0)
    flipped = 7 - sub
    spread = lax.broadcasted_iota(jnp.int32, (LANES, LANES), 0)
    counting = (lane + 1).astype(jnp.float32)

    level = eight(ints_ref[0:1])
    neighbour = eight(ints_ref[1:2])
    coarse_index = eight(ints_ref[2:3])
    quadrant = eight(ints_ref[3:4])
    fine_index = eight(ints_ref[4:5])
    turns = eight(ints_ref[5:6])
    coarse_live = eight(ints_ref[6:7]) > 0
    fine_live = eight(ints_ref[7:8]) > 0
    metric = jnp.where(level == 0, 1.0, jnp.where(level == 1, 2.0, 4.0))
    own_a = quadrant >= 2
    own_c = quadrant % 2 == 1
    back_turns = (4 - turns) % 4

    def inverse_of(row, counts):
        table = jnp.where(spread == row, 1.0, 0.0).astype(jnp.bfloat16)
        found = lax.dot_general(
            counts.astype(jnp.bfloat16), table, (((1,), (1,)), ((), ())),
            preferred_element_type=jnp.float32,
        )
        present = found > 0.5
        return jnp.maximum(found - 1.0, 0.0).astype(jnp.int32), present

    x_source, _ = inverse_of(ints_ref[1:2], counting)
    c_source, c_present = inverse_of(
        ints_ref[2:3], jnp.where(lane % 4 == 0, counting, 0.0)
    )
    f_source, f_present = inverse_of(ints_ref[4:5], counting)
    group_pick = (lane // 32) * 32 + (lane % 8) * 4
    group_index = lane_pick(coarse_index, group_pick)
    group_block = (lane // 8) % 4
    widen = [(lane // 32) * 32 + k * 8 + (lane % 32) // 4 for k in range(4)]

    def rev(x):
        return jnp.take_along_axis(x, flipped, axis=0, mode="promise_in_bounds")

    def rotated(ref, v, amount):
        odd = amount % 2 == 1
        far = amount >= 2
        mixed = [
            jnp.where(odd, ref[v, pl.ds(7 - i, 8, stride=8), :], ref[v, pl.ds(8 * i, 8), :])
            for i in range(8)
        ]
        return [jnp.where(far, rev(mixed[7 - i]), mixed[i]) for i in range(8)]

    def half_both(matrix, upper_a, upper_c, values, v):
        along_a = half_map(matrix, upper_a, values)
        for i in range(8):
            work[v, pl.ds(8 * i, 8), :] = along_a[i]
        columns = [work[v, pl.ds(j, 8, stride=8), :] for j in range(8)]
        return half_map(matrix, upper_c, columns)

    def send_mortars(state, stage):
        def one(v, carry):
            top = [state[v, pl.ds(64 * a + 56, 8), :] for a in range(8)]
            for h in range(2):
                pack = lane_pick(top[4 * h], group_index)
                for k in range(1, 4):
                    pack = jnp.where(group_block == k, lane_pick(top[4 * h + k], group_index), pack)
                packed[2 * v + h] = pack
            for a in range(8):
                work[v, pl.ds(8 * a, 8), :] = lane_pick(state[v, pl.ds(64 * a, 8), :], fine_index)
            turned = rotated(work, v, back_turns)
            for a in range(8):
                own_fine[v, pl.ds(8 * a, 8), :] = turned[a]
            for h in range(2):
                blocks = swap_blocks(turned[4 * h : 4 * h + 4], lane)
                for o in range(OFFS):
                    fsend[stage, o, tile(2 * v + h), :] = blocks[o]
            return carry

        lax.fori_loop(0, NVAR, one, 0)
        packed[10] = quadrant.astype(jnp.float32)
        packed[11] = jnp.zeros((8, LANES), jnp.float32)
        for m in range(3):
            blocks = swap_blocks([packed[4 * m + k] for k in range(4)], lane)
            for o in range(OFFS):
                csend[stage, o, pl.ds(8 * m, 8), :] = blocks[o]

    def mortar_copies(stage):
        copies = []
        for o in range(OFFS):
            copies.append(pltpu.make_async_remote_copy(
                src_ref=fsend.at[stage, o], dst_ref=frecv.at[stage, o],
                send_sem=fs_sem.at[stage, o], recv_sem=fr_sem.at[stage, o],
                device_id=back[o], device_id_type=MESH))
            copies.append(pltpu.make_async_remote_copy(
                src_ref=csend.at[stage, o], dst_ref=crecv.at[stage, o],
                send_sem=cs_sem.at[stage, o], recv_sem=cr_sem.at[stage, o],
                device_id=ahead[o], device_id_type=MESH))
        return copies

    def z_copies(stage):
        targets = [(s, (t + 1) % cuts), (s, (t + cuts - 1) % cuts)]
        return [
            pltpu.make_async_remote_copy(
                src_ref=zsend.at[stage, i], dst_ref=zrecv.at[stage, i],
                send_sem=zs_sem.at[stage, i], recv_sem=zr_sem.at[stage, i],
                device_id=targets[i], device_id_type=MESH)
            for i in range(2)
        ]

    def z_traces(state, stage):
        for v in range(NVAR):
            zsend[stage, 0, v] = state[v, pl.ds(7, FACE, stride=8), :]
            zsend[stage, 1, v] = state[v, pl.ds(0, FACE, stride=8), :]

    def own_interpolated(state):
        def one(v, carry):
            picked = [lane_pick(state[v, pl.ds(64 * a + 56, 8), :], coarse_index) for a in range(8)]
            columns = half_both(HALF, own_a, own_c, picked, v)
            for j in range(8):
                own_coarse[v, pl.ds(j, 8, stride=8), :] = columns[j]
            return carry

        lax.fori_loop(0, NVAR, one, 0)

    def primitive_pass(state, with_speed):
        def one(i, fastest):
            rows = pl.ds(pl.multiple_of(i * 32, 32), 32)
            u = [state[v, rows, :] for v in range(NVAR)]
            inverse, velocity, pressure = primitives(u)
            for d in range(3):
                prim[d, rows, :] = velocity[d]
            prim[3, rows, :] = pressure
            if not with_speed:
                return fastest
            square = velocity[0] * velocity[0] + velocity[1] * velocity[1] + velocity[2] * velocity[2]
            speed = jnp.sqrt(square) + jnp.sqrt(1.4 * pressure * inverse)
            return jnp.maximum(fastest, speed)

        start = jnp.zeros((32, LANES) if with_speed else (8, LANES), jnp.float32)
        return lax.fori_loop(0, 16, one, start)

    def volume(state):
        def line(read, normal, pressure, direction, v):
            if v == 0:
                return [read(1 + direction, j) for j in range(8)]
            if v == 4:
                return [normal[j] * (read(4, j) + pressure[j]) for j in range(8)]
            if v == 1 + direction:
                return [read(v, j) * normal[j] + pressure[j] for j in range(8)]
            return [read(v, j) * normal[j] for j in range(8)]

        def z_pass(a, carry):
            def at(j):
                return pl.ds(a * 64 + j, 8, stride=8)

            normal = [prim[2, at(j), :] for j in range(8)]
            pressure = [prim[3, at(j), :] for j in range(8)]
            for v in range(NVAR):
                out = derive(line(lambda w, j: state[w, at(j), :], normal, pressure, 2, v))
                for j in range(8):
                    rate[v, at(j), :] = out[j]
            return carry

        def y_pass(a, carry):
            def at(j):
                return pl.ds(pl.multiple_of(a * 64 + j * 8, 8), 8)

            normal = [prim[1, at(j), :] for j in range(8)]
            pressure = [prim[3, at(j), :] for j in range(8)]
            for v in range(NVAR):
                out = derive(line(lambda w, j: state[w, at(j), :], normal, pressure, 1, v))
                for j in range(8):
                    rate[v, at(j), :] += out[j]
            return carry

        def x_pass(b, carry):
            def at(j):
                return pl.ds(pl.multiple_of(b * 8 + j * 64, 8), 8)

            normal = [prim[0, at(j), :] for j in range(8)]
            pressure = [prim[3, at(j), :] for j in range(8)]
            for v in range(NVAR):
                out = derive(line(lambda w, j: state[w, at(j), :], normal, pressure, 0, v))
                for j in range(8):
                    rate[v, at(j), :] += out[j]
            return carry

        lax.fori_loop(0, 8, z_pass, 0)
        lax.fori_loop(0, 8, y_pass, 0)
        lax.fori_loop(0, 8, x_pass, 0)

    def x_faces(state):
        def one(i, carry):
            low = pl.ds(pl.multiple_of(i * 16, 16), 16)
            high = pl.ds(pl.multiple_of(448 + i * 16, 16), 16)
            pick = jnp.broadcast_to(ints_ref[1:2], (16, LANES))
            source = jnp.concatenate([x_source, x_source], axis=0)
            left = [state[v, high, :] for v in range(NVAR)]
            right = [lane_pick(state[v, low, :], pick) for v in range(NVAR)]
            mean, jump = face_parts(left, right, 0)
            for v in range(NVAR):
                rate[v, high, :] += LIFT * (mean[v] - jump[v])
                rate[v, low, :] += LIFT * lane_pick(mean[v] + jump[v], source)
            return carry

        lax.fori_loop(0, 4, one, 0)

    def z_faces(stage):
        def one(i, carry):
            rows = pl.ds(pl.multiple_of(i * 16, 16), 16)
            bottom = pl.ds(i * 128, 16, stride=8)
            top = pl.ds(i * 128 + 7, 16, stride=8)
            left = [zsend[stage, 0, v, rows, :] for v in range(NVAR)]
            right = [zrecv[stage, 1, v, rows, :] for v in range(NVAR)]
            mean, jump = face_parts(left, right, 2)
            for v in range(NVAR):
                rate[v, top, :] += LIFT * (mean[v] - jump[v])
            left = [zrecv[stage, 0, v, rows, :] for v in range(NVAR)]
            right = [zsend[stage, 1, v, rows, :] for v in range(NVAR)]
            mean, jump = face_parts(left, right, 2)
            for v in range(NVAR):
                rate[v, bottom, :] += LIFT * (mean[v] + jump[v])
            return carry

        lax.fori_loop(0, 4, one, 0)

    def mortars(stage):
        for m in range(3):
            blocks = swap_blocks([crecv[stage, o, pl.ds(8 * m, 8), :] for o in range(OFFS)], lane)
            for k in range(4):
                packed[4 * m + k] = blocks[k]
        far_quadrant = packed[10]
        far_a = far_quadrant > 1.5
        far_c = (far_quadrant == 1.0) | (far_quadrant == 3.0)

        def expand(v, carry):
            for h in range(2):
                blocks = swap_blocks([frecv[stage, o, tile(2 * v + h), :] for o in range(OFFS)], lane)
                for k in range(4):
                    far_fine[v, pl.ds(8 * (4 * h + k), 8), :] = blocks[k]
            picked = [lane_pick(packed[2 * v + a // 4], widen[a % 4]) for a in range(8)]
            columns = half_both(HALF, far_a, far_c, picked, v)
            for j in range(8):
                far_coarse[v, pl.ds(j, 8, stride=8), :] = columns[j]
            return carry

        lax.fori_loop(0, NVAR, expand, 0)

        def fluxes(i, carry):
            rows = pl.ds(pl.multiple_of(i * 16, 16), 16)
            live = jnp.concatenate([coarse_live, coarse_live], axis=0)
            left = [own_coarse[v, rows, :] for v in range(NVAR)]
            right = [far_fine[v, rows, :] for v in range(NVAR)]
            mean, jump = face_parts(left, right, 1)
            for v in range(NVAR):
                own_coarse[v, rows, :] = jnp.where(live, mean[v] - jump[v], 0.0)
            live = jnp.concatenate([fine_live, fine_live], axis=0)
            left = [far_coarse[v, rows, :] for v in range(NVAR)]
            right = [own_fine[v, rows, :] for v in range(NVAR)]
            mean, jump = face_parts(left, right, 1)
            for v in range(NVAR):
                own_fine[v, rows, :] = jnp.where(live, mean[v] + jump[v], 0.0)
            return carry

        lax.fori_loop(0, 4, fluxes, 0)

        def scatter(v, carry):
            values = [own_coarse[v, pl.ds(8 * a, 8), :] for a in range(8)]
            columns = half_both(BACK, own_a, own_c, values, v)
            for c in range(8):
                total = columns[c] + pltpu.roll(columns[c], 127, 1)
                total = total + pltpu.roll(total, 126, 1)
                share = jnp.where(c_present, lane_pick(total, c_source), 0.0)
                rate[v, pl.ds(56 + c, 8, stride=64), :] += LIFT * share
            turned = rotated(own_fine, v, turns)
            for a in range(8):
                share = jnp.where(f_present, lane_pick(turned[a], f_source), 0.0)
                rate[v, pl.ds(64 * a, 8), :] += LIFT * share
            return carry

        lax.fori_loop(0, NVAR, scatter, 0)

    def speed_round(first, peers):
        return [
            pltpu.make_async_remote_copy(
                src_ref=vsend.at[0 if first == 0 else (1 if first == cuts - 1 else 2)],
                dst_ref=vrecv.at[first + i],
                send_sem=vs_sem.at[first + i], recv_sem=vr_sem.at[first + i],
                device_id=peer, device_id_type=MESH)
            for i, peer in enumerate(peers)
        ]

    def finish_round(copies, value, first):
        for copy in copies:
            copy.wait_recv()
        for i in range(len(copies)):
            value = jnp.maximum(value, vrecv[first + i])
        return value

    speed = primitive_pass(u_ref, True)
    speed = jnp.maximum(jnp.maximum(speed[0:8], speed[8:16]), jnp.maximum(speed[16:24], speed[24:32]))
    speed = speed * metric
    vsend[0] = speed
    pl.semaphore_wait(barrier, len(greeted))
    round_1 = speed_round(0, cut_peers)
    for copy in round_1:
        copy.start()
    started = list(round_1)
    z_traces(u_ref, 0)
    zc = z_copies(0)
    for copy in zc:
        copy.start()
    send_mortars(u_ref, 0)
    mc = mortar_copies(0)
    for copy in mc:
        copy.start()
    started += zc + mc
    own_interpolated(u_ref)
    speed = finish_round(round_1, speed, 0)
    vsend[1] = speed
    round_2 = speed_round(cuts - 1, y_peers)
    for copy in round_2:
        copy.start()
    started += round_2
    volume(u_ref)
    speed = finish_round(round_2, speed, cuts - 1)
    vsend[2] = speed
    round_3 = speed_round(cuts + ys - 2, z_peers)
    for copy in round_3:
        copy.start()
    started += round_3
    x_faces(u_ref)
    for copy in zc:
        copy.wait_recv()
    z_faces(0)
    for copy in mc:
        copy.wait_recv()
    mortars(0)
    speed = finish_round(round_3, speed, cuts + ys - 2)
    step = 0.005 / jnp.broadcast_to(jnp.max(speed, keepdims=True), (8, LANES))
    scale = -(metric * step)
    scale = jnp.concatenate([scale] * 4, axis=0)

    def first_update(i, carry):
        rows = pl.ds(pl.multiple_of(i * 32, 32), 32)
        for v in range(NVAR):
            change = scale * rate[v, rows, :]
            reg_ref[v, rows, :] = change
            sect[v, rows, :] = u_ref[v, rows, :] + section_b[0] * change
        return carry

    lax.fori_loop(0, 16, first_update, 0)

    z_traces(sect, 1)
    zc = z_copies(1)
    for copy in zc:
        copy.start()
    send_mortars(sect, 1)
    mc = mortar_copies(1)
    for copy in mc:
        copy.start()
    started += zc + mc
    own_interpolated(sect)
    primitive_pass(sect, False)
    volume(sect)
    x_faces(sect)
    for copy in zc:
        copy.wait_recv()
    z_faces(1)
    for copy in mc:
        copy.wait_recv()
    mortars(1)

    def second_update(i, carry):
        rows = pl.ds(pl.multiple_of(i * 32, 32), 32)
        for v in range(NVAR):
            register = section_a[1] * reg_ref[v, rows, :] + scale * rate[v, rows, :]
            reg_ref[v, rows, :] = register
            adv_ref[v, rows, :] = sect[v, rows, :] + section_b[1] * register
        return carry

    lax.fori_loop(0, 16, second_update, 0)
    for copy in started:
        copy.wait_send()


def on_device(
    slabs, cuts, ys, zs,
    conserved,
    refinement,
    x_neighbour,
    coarse_element,
    quadrant,
    send_count,
    fine_element,
    orientation,
    receive_count,
):
    slots = jnp.arange(CAP, dtype=jnp.int32)[None, :]
    coarse_live = (slots < send_count.reshape(OFFS, 1)).astype(jnp.int32)
    fine_live = (slots < receive_count.reshape(OFFS, 1)).astype(jnp.int32)
    ints = jnp.stack([
        row.reshape(LANES)
        for row in (
            refinement, x_neighbour, coarse_element, quadrant,
            fine_element, orientation, coarse_live, fine_live,
        )
    ])
    peers = cuts + ys + zs - 3
    state = (NVAR, NP * FACE, LANES)
    face = (NVAR, FACE, LANES)
    return pl.pallas_call(
        functools.partial(kernel, slabs, cuts, ys, zs),
        out_shape=[jax.ShapeDtypeStruct(state, jnp.float32)] * 2,
        in_specs=[pl.BlockSpec(memory_space=pltpu.VMEM)] * 2,
        out_specs=[pl.BlockSpec(memory_space=pltpu.VMEM)] * 2,
        scratch_shapes=[
            pltpu.VMEM((4, NP * FACE, LANES), jnp.float32),
            pltpu.VMEM(state, jnp.float32),
            pltpu.VMEM(state, jnp.float32),
            pltpu.VMEM((2, 2) + face, jnp.float32),
            pltpu.VMEM((2, 2) + face, jnp.float32),
            pltpu.VMEM((2, OFFS, 24, LANES), jnp.float32),
            pltpu.VMEM((2, OFFS, 24, LANES), jnp.float32),
            pltpu.VMEM((2, OFFS, 80, LANES), jnp.float32),
            pltpu.VMEM((2, OFFS, 80, LANES), jnp.float32),
            pltpu.VMEM((3, 8, LANES), jnp.float32),
            pltpu.VMEM((peers, 8, LANES), jnp.float32),
            pltpu.VMEM(face, jnp.float32),
            pltpu.VMEM(face, jnp.float32),
            pltpu.VMEM(face, jnp.float32),
            pltpu.VMEM(face, jnp.float32),
            pltpu.VMEM(face, jnp.float32),
            pltpu.VMEM((12, 8, LANES), jnp.float32),
            pltpu.SemaphoreType.DMA((2, 2)),
            pltpu.SemaphoreType.DMA((2, 2)),
            pltpu.SemaphoreType.DMA((2, OFFS)),
            pltpu.SemaphoreType.DMA((2, OFFS)),
            pltpu.SemaphoreType.DMA((2, OFFS)),
            pltpu.SemaphoreType.DMA((2, OFFS)),
            pltpu.SemaphoreType.DMA((peers,)),
            pltpu.SemaphoreType.DMA((peers,)),
        ],
        compiler_params=pltpu.CompilerParams(
            collective_id=0, has_side_effects=True, vmem_limit_bytes=40 * 1024 * 1024
        ),
    )(conserved, ints)


def solution(mesh):
    slabs, cuts = mesh.shape["slab"], mesh.shape["cut"]
    zs = 12 if slabs % 12 == 0 else 3
    return jax.shard_map(
        functools.partial(on_device, slabs, cuts, slabs // zs, zs),
        mesh=mesh,
        in_specs=(
            P(None, None, ("slab", "cut")),
            P(("slab", "cut")),
            P(("slab", "cut"), None),
            P("slab", "cut", None, None),
            P("slab", "cut", None, None),
            P("slab", "cut", None),
            P("slab", "cut", None, None),
            P("slab", "cut", None, None),
            P("slab", "cut", None),
        ),
        out_specs=(P(None, None, ("slab", "cut")), P(None, None, ("slab", "cut"))),
        check_vma=False,
    )
```

```python
import functools

import jax
import jax.numpy as jnp
import numpy as np
from jax import lax
from jax.experimental import pallas as pl
from jax.experimental.pallas import tpu as pltpu
from jax.sharding import PartitionSpec as P

NP = 8
NVAR = 5
FACE = NP * NP
LANES = 128
OFFS = 4
CAP = 32
UNROLL_SEND = NVAR
UNROLL_OWN = NVAR
UNROLL_EXPAND = NVAR
UNROLL_SCATTER = NVAR
UNROLL_FACE = 4
UNROLL_VOLUME = 2
UNROLL_UPDATE = 4
MESH = pl.DeviceIdType.MESH

section_a = (0.0, -567301805773.0 / 1357537059087.0)
section_b = (1432997174477.0 / 9575080441755.0, 5161836677717.0 / 13612068292357.0)


def legendre_rows(points, node_count):
    legendre = np.zeros((node_count, node_count))
    legendre[:, 0] = 1.0
    legendre[:, 1] = points
    for degree in range(2, node_count):
        legendre[:, degree] = (
            (2 * degree - 1) * points * legendre[:, degree - 1]
            - (degree - 1) * legendre[:, degree - 2]
        ) / degree
    return legendre


def lobatto(node_count):
    poly_order = node_count - 1
    points = -np.cos(np.pi * np.arange(node_count) / poly_order)
    for newton_step in range(40):
        legendre = legendre_rows(points, node_count)
        points = points - (points * legendre[:, poly_order] - legendre[:, poly_order - 1]) / (
            node_count * legendre[:, poly_order]
        )
    top_row = legendre_rows(points, node_count)[:, poly_order]
    weights = 2.0 / (poly_order * node_count * top_row * top_row)
    differ = np.zeros((node_count, node_count))
    for target in range(node_count):
        for source in range(node_count):
            if target != source:
                differ[target, source] = top_row[target] / (
                    top_row[source] * (points[target] - points[source])
                )
    differ[0, 0] = -poly_order * node_count / 4.0
    differ[poly_order, poly_order] = poly_order * node_count / 4.0
    lower_half = np.zeros((node_count, node_count))
    targets = (points - 1) / 2.0
    for source in range(node_count):
        basis = np.ones(node_count)
        for other in range(node_count):
            if other != source:
                basis = basis * (targets - points[other]) / (points[source] - points[other])
        lower_half[:, source] = basis
    lower_back = 0.5 * np.transpose(lower_half) * weights[None, :] / weights[:, None]
    return (weights, differ, lower_half, lower_back)


WEIGHTS, DIFFER, HALF, BACK = lobatto(NP)
LIFT = float(1.0 / WEIGHTS[0])
EVEN = 0.5 * (DIFFER[:4, :4] + DIFFER[:4, :3:-1])
ODD = 0.5 * (DIFFER[:4, :4] - DIFFER[:4, :3:-1])


def combine(row, values):
    total = None
    for weight, value in zip(row, values):
        weight = float(np.float32(weight))
        if abs(weight) < 1e-12:
            continue
        term = value if weight == 1.0 else weight * value
        total = term if total is None else total + term
    return total


def derive(f):
    even = [f[j] + f[7 - j] for j in range(4)]
    odd = [f[j] - f[7 - j] for j in range(4)]
    out = [None] * 8
    for i in range(4):
        from_even = combine(EVEN[i], even)
        from_odd = combine(ODD[i], odd)
        out[i] = from_odd + from_even
        out[7 - i] = from_odd - from_even
    return out


def half_map(matrix, upper, f):
    f = [jnp.where(upper, f[7 - j], f[j]) for j in range(8)]
    g = [combine(matrix[i], f) for i in range(8)]
    return [jnp.where(upper, g[7 - i], g[i]) for i in range(8)]


def primitives(u):
    inverse = 1.0 / u[0]
    velocity = [u[1] * inverse, u[2] * inverse, u[3] * inverse]
    carried = u[1] * velocity[0] + u[2] * velocity[1] + u[3] * velocity[2]
    pressure = 0.4 * (u[4] - 0.5 * carried)
    return inverse, velocity, pressure


def flux_of(u, normal, pressure, direction):
    rows = [u[1 + direction]]
    for column in range(3):
        carried = u[1 + column] * normal
        rows.append(carried + pressure if column == direction else carried)
    rows.append(normal * (u[4] + pressure))
    return rows


def face_flux(u, direction):
    inverse, velocity, pressure = primitives(u)
    normal = velocity[direction]
    speed = jnp.abs(normal) + jnp.sqrt(1.4 * pressure * inverse)
    return flux_of(u, normal, pressure, direction), speed


def face_parts(left, right, direction):
    left_flux, left_speed = face_flux(left, direction)
    right_flux, right_speed = face_flux(right, direction)
    half_speed = 0.5 * jnp.maximum(left_speed, right_speed)
    mean = [0.5 * (r - l) for l, r in zip(left_flux, right_flux)]
    jump = [half_speed * (r - l) for l, r in zip(left, right)]
    return mean, jump


def lane_pick(x, index):
    return jnp.take_along_axis(x, index, axis=1, mode="promise_in_bounds")


def swap_blocks(x, lane):
    high = lane >= 64
    odd = (lane // 32) % 2 == 1
    y = list(x)
    for k in (0, 1):
        y[k] = jnp.where(high, pltpu.roll(x[k + 2], 64, 1), x[k])
        y[k + 2] = jnp.where(high, x[k + 2], pltpu.roll(x[k], 64, 1))
    z = list(y)
    for k in (0, 2):
        z[k] = jnp.where(odd, pltpu.roll(y[k + 1], 32, 1), y[k])
        z[k + 1] = jnp.where(odd, y[k + 1], pltpu.roll(y[k], 96, 1))
    return z


def offset_distance(offset_index):
    return (offset_index // 2 + 1) * (1 - 2 * (offset_index % 2))


def eight(row):
    return jnp.broadcast_to(row, (8, LANES))


def tile(i):
    return pl.ds(pl.multiple_of(i * 8, 8), 8)


def loop(count, body, unroll):
    def step(i, carry):
        body(i)
        return carry

    lax.fori_loop(0, count, step, 0, unroll=unroll)


def kernel(
    slabs, cuts, ys, zs,
    u_hbm, ints_ref,
    adv_ref, reg_ref,
    u,
    prim, rate, sect,
    zsend, zrecv, csend, crecv, fsend, frecv,
    vsend, vrecv,
    own_coarse, own_fine, far_coarse, far_fine, coarse_term, fine_term, work, packed,
    in_sem, zs_sem, zr_sem, cs_sem, cr_sem, fs_sem, fr_sem, vs_sem, vr_sem,
):
    s = lax.axis_index("slab")
    t = lax.axis_index("cut")
    y = s // zs
    z = s % zs
    cut_peers = [(s, (t + d) % cuts) for d in range(1, cuts)]
    y_peers = [(((y + d) % ys) * zs + z, t) for d in range(1, ys)]
    z_peers = [(y * zs + (z + d) % zs, t) for d in range(1, zs)]
    ahead = [((s + offset_distance(o) + slabs) % slabs, t) for o in range(OFFS)]
    back = [((s - offset_distance(o) + slabs) % slabs, t) for o in range(OFFS)]

    loads = [
        pltpu.make_async_copy(
            u_hbm.at[:, pl.ds(64 * a, 64), :], u.at[:, pl.ds(64 * a, 64), :], in_sem.at[a]
        )
        for a in range(8)
    ]
    for copy in loads:
        copy.start()

    barrier = pltpu.get_barrier_semaphore()
    greeted = cut_peers + y_peers + z_peers + ahead
    for peer in greeted:
        pl.semaphore_signal(barrier, inc=1, device_id=peer, device_id_type=MESH)

    lane = lax.broadcasted_iota(jnp.int32, (8, LANES), 1)
    sub = lax.broadcasted_iota(jnp.int32, (8, LANES), 0)
    flipped = 7 - sub
    block = lane // CAP
    spread = lax.broadcasted_iota(jnp.int32, (LANES, LANES), 0)
    counting = (lane + 1).astype(jnp.float32)

    level = eight(ints_ref[0:1])
    metric = jnp.where(level == 0, 1.0, jnp.where(level == 1, 2.0, 4.0))
    negative = -metric

    fastest = jnp.zeros((32, LANES), jnp.float32)
    for a in range(8):
        loads[a].wait()

        def one(i, fastest):
            rows = pl.ds(pl.multiple_of(64 * a + i * 32, 32), 32)
            state = [u[v, rows, :] for v in range(NVAR)]
            inverse, velocity, pressure = primitives(state)
            for d in range(3):
                prim[d, rows, :] = velocity[d]
            prim[3, rows, :] = pressure
            square = velocity[0] * velocity[0] + velocity[1] * velocity[1] + velocity[2] * velocity[2]
            return jnp.maximum(fastest, jnp.sqrt(square) + jnp.sqrt(1.4 * pressure * inverse))

        fastest = lax.fori_loop(0, 2, one, fastest, unroll=True)
    speed = jnp.maximum(jnp.maximum(fastest[0:8], fastest[8:16]), jnp.maximum(fastest[16:24], fastest[24:32]))
    speed = jnp.max(speed * metric, axis=0, keepdims=True)
    vsend[0, 0:1] = speed

    def speed_round(number, first, peers):
        return [
            pltpu.make_async_remote_copy(
                src_ref=vsend.at[number, pl.ds(0, 1)], dst_ref=vrecv.at[first + i, pl.ds(0, 1)],
                send_sem=vs_sem.at[first + i], recv_sem=vr_sem.at[first + i],
                device_id=peer, device_id_type=MESH)
            for i, peer in enumerate(peers)
        ]

    def finish_round(copies, value, first):
        for copy in copies:
            copy.wait_recv()
        for i in range(len(copies)):
            value = jnp.maximum(value, vrecv[first + i, 0:1])
        return value

    round_1 = speed_round(0, 0, cut_peers)
    round_2 = speed_round(1, cuts - 1, y_peers)
    round_3 = speed_round(2, cuts + ys - 2, z_peers)

    def z_copies(stage):
        targets = [(s, (t + 1) % cuts), (s, (t + cuts - 1) % cuts)]
        return [
            pltpu.make_async_remote_copy(
                src_ref=zsend.at[stage, i], dst_ref=zrecv.at[stage, i],
                send_sem=zs_sem.at[stage, i], recv_sem=zr_sem.at[stage, i],
                device_id=targets[i], device_id_type=MESH)
            for i in range(2)
        ]

    def fine_copies(stage):
        return [
            pltpu.make_async_remote_copy(
                src_ref=fsend.at[stage, o], dst_ref=frecv.at[stage, o],
                send_sem=fs_sem.at[stage, o], recv_sem=fr_sem.at[stage, o],
                device_id=back[o], device_id_type=MESH)
            for o in range(OFFS)
        ]

    def coarse_copies(stage):
        return [
            pltpu.make_async_remote_copy(
                src_ref=csend.at[stage, o], dst_ref=crecv.at[stage, o],
                send_sem=cs_sem.at[stage, o], recv_sem=cr_sem.at[stage, o],
                device_id=ahead[o], device_id_type=MESH)
            for o in range(OFFS)
        ]

    pl.semaphore_wait(barrier, len(greeted))
    for copy in round_1:
        copy.start()

    def z_traces(read, stage):
        for v in range(NVAR):
            zsend[stage, 0, v] = read(v, pl.ds(7, FACE, stride=8))
            zsend[stage, 1, v] = read(v, pl.ds(0, FACE, stride=8))

    def read_state(v, rows):
        return u[v, rows, :]

    def read_rate(v, rows):
        values = rate[v, rows, :]
        return jnp.broadcast_to(negative[0:1], values.shape) * values

    z_first = z_copies(0)
    z_traces(read_state, 0)
    for copy in z_first:
        copy.start()

    def row_of(first):
        parts = [ints_ref[first + o : first + o + 1, 0:CAP] for o in range(OFFS)]
        return eight(jnp.concatenate(parts, axis=1))

    def live_of(row):
        count = jnp.broadcast_to(ints_ref[row : row + 1, 0:1], (8, LANES))
        for o in range(1, OFFS):
            count = jnp.where(block == o, jnp.broadcast_to(ints_ref[row : row + 1, o : o + 1], (8, LANES)), count)
        return lane % CAP < count

    neighbour = eight(ints_ref[8:9])
    coarse_index = row_of(16)
    quadrant = row_of(24)
    fine_index = row_of(32)
    turns = row_of(40)
    coarse_live = live_of(48)
    fine_live = live_of(56)
    own_a = quadrant >= 2
    own_c = quadrant % 2 == 1
    back_turns = (4 - turns) % 4
    group_pick = block * CAP + (lane % 8) * 4
    group_index = lane_pick(coarse_index, group_pick)
    group_block = (lane // 8) % 4
    widen = [block * CAP + k * 8 + (lane % CAP) // 4 for k in range(4)]

    def rev(x):
        return jnp.take_along_axis(x, flipped, axis=0, mode="promise_in_bounds")

    def rotated(read, amount):
        odd = amount % 2 == 1
        far = amount >= 2
        mixed = [
            jnp.where(odd, read(pl.ds(7 - i, 8, stride=8)), read(pl.ds(8 * i, 8)))
            for i in range(8)
        ]
        return [jnp.where(far, rev(mixed[7 - i]), mixed[i]) for i in range(8)]

    def half_both(matrix, upper_a, upper_c, values, v):
        along_a = half_map(matrix, upper_a, values)
        for i in range(8):
            work[v, pl.ds(8 * i, 8), :] = along_a[i]
        columns = [work[v, pl.ds(j, 8, stride=8), :] for j in range(8)]
        return half_map(matrix, upper_c, columns)

    def send_mortars(read, stage, fine, coarse):
        def fine_side(v):
            for a in range(8):
                work[v, pl.ds(8 * a, 8), :] = lane_pick(read(v, pl.ds(64 * a, 8)), fine_index)
            turned = rotated(lambda rows: work[v, rows, :], back_turns)
            for a in range(8):
                own_fine[stage, v, pl.ds(8 * a, 8), :] = turned[a]
            for h in range(2):
                blocks = swap_blocks(turned[4 * h : 4 * h + 4], lane)
                for o in range(OFFS):
                    fsend[stage, o, tile(2 * v + h), :] = blocks[o]

        loop(NVAR, fine_side, UNROLL_SEND)
        for copy in fine:
            copy.start()

        def coarse_side(v):
            for h in range(2):
                pack = lane_pick(read(v, pl.ds(256 * h + 56, 8)), group_index)
                for k in range(1, 4):
                    top = read(v, pl.ds(256 * h + 64 * k + 56, 8))
                    pack = jnp.where(group_block == k, lane_pick(top, group_index), pack)
                packed[2 * v + h] = pack

        loop(NVAR, coarse_side, UNROLL_SEND)
        packed[10] = quadrant.astype(jnp.float32)
        packed[11] = jnp.zeros((8, LANES), jnp.float32)
        for m in range(3):
            blocks = swap_blocks([packed[4 * m + k] for k in range(4)], lane)
            for o in range(OFFS):
                csend[stage, o, pl.ds(8 * m, 8), :] = blocks[o]
        for copy in coarse:
            copy.start()

    def own_interpolated(read, stage):
        def one(v):
            picked = [lane_pick(read(v, pl.ds(64 * a + 56, 8)), coarse_index) for a in range(8)]
            columns = half_both(HALF, own_a, own_c, picked, v)
            for j in range(8):
                own_coarse[stage, v, pl.ds(j, 8, stride=8), :] = columns[j]

        loop(NVAR, one, UNROLL_OWN)

    def line(read, normal, pressure, direction, v):
        if v == 0:
            return [read(1 + direction, j) for j in range(8)]
        if v == 4:
            return [normal[j] * (read(4, j) + pressure[j]) for j in range(8)]
        if v == 1 + direction:
            return [read(v, j) * normal[j] + pressure[j] for j in range(8)]
        return [read(v, j) * normal[j] for j in range(8)]

    def volume(state, direction, at, fresh):
        def one(i):
            normal = [prim[direction, at(i, j), :] for j in range(8)]
            pressure = [prim[3, at(i, j), :] for j in range(8)]
            for v in range(NVAR):
                out = derive(line(lambda w, j: state[w, at(i, j), :], normal, pressure, direction, v))
                for j in range(8):
                    if fresh:
                        rate[v, at(i, j), :] = out[j]
                    else:
                        rate[v, at(i, j), :] += out[j]

        loop(8, one, UNROLL_VOLUME)

    def volume_z(state):
        volume(state, 2, lambda a, j: pl.ds(a * 64 + j, 8, stride=8), True)

    def volume_y(state):
        volume(state, 1, lambda a, j: pl.ds(pl.multiple_of(a * 64 + j * 8, 8), 8), False)

    def volume_x(state):
        volume(state, 0, lambda b, j: pl.ds(pl.multiple_of(b * 8 + j * 64, 8), 8), False)

    def inverse_of(row, counts):
        table = jnp.where(spread == row, 1.0, 0.0).astype(jnp.bfloat16)
        found = lax.dot_general(
            counts.astype(jnp.bfloat16), table, (((1,), (1,)), ((), ())),
            preferred_element_type=jnp.float32,
        )
        present = found > 0.5
        return jnp.maximum(found - 1.0, 0.0).astype(jnp.int32), present

    x_source, _ = inverse_of(neighbour[0:1], counting)
    c_source, c_present = inverse_of(coarse_index[0:1], jnp.where(lane % 4 == 0, counting, 0.0))
    f_source, f_present = inverse_of(fine_index[0:1], counting)

    def x_faces(state):
        def one(i):
            low = pl.ds(pl.multiple_of(i * 16, 16), 16)
            high = pl.ds(pl.multiple_of(448 + i * 16, 16), 16)
            pick = jnp.broadcast_to(neighbour[0:1], (16, LANES))
            source = jnp.broadcast_to(x_source[0:1], (16, LANES))
            left = [state[v, high, :] for v in range(NVAR)]
            right = [lane_pick(state[v, low, :], pick) for v in range(NVAR)]
            mean, jump = face_parts(left, right, 0)
            for v in range(NVAR):
                rate[v, high, :] += LIFT * (mean[v] - jump[v])
                rate[v, low, :] += LIFT * lane_pick(mean[v] + jump[v], source)

        loop(4, one, UNROLL_FACE)

    def blend(ref, index, factor):
        if factor is None:
            return ref[(0,) + index]
        first = ref[(0,) + index]
        return first + jnp.broadcast_to(factor, first.shape) * ref[(1,) + index]

    def z_faces(factor):
        def one(i):
            rows = pl.ds(pl.multiple_of(i * 16, 16), 16)
            bottom = pl.ds(i * 128, 16, stride=8)
            top = pl.ds(i * 128 + 7, 16, stride=8)
            left = [blend(zsend, (0, v, rows, slice(None)), factor) for v in range(NVAR)]
            right = [blend(zrecv, (1, v, rows, slice(None)), factor) for v in range(NVAR)]
            mean, jump = face_parts(left, right, 2)
            for v in range(NVAR):
                rate[v, top, :] += LIFT * (mean[v] - jump[v])
            left = [blend(zrecv, (0, v, rows, slice(None)), factor) for v in range(NVAR)]
            right = [blend(zsend, (1, v, rows, slice(None)), factor) for v in range(NVAR)]
            mean, jump = face_parts(left, right, 2)
            for v in range(NVAR):
                rate[v, bottom, :] += LIFT * (mean[v] + jump[v])

        loop(4, one, UNROLL_FACE)

    def far_quadrants():
        far = packed[10]
        return far > 1.5, (far == 1.0) | (far == 3.0)

    def expand(stage):
        for m in range(3):
            blocks = swap_blocks([crecv[stage, o, pl.ds(8 * m, 8), :] for o in range(OFFS)], lane)
            for k in range(4):
                packed[4 * m + k] = blocks[k]
        far_a, far_c = far_quadrants()

        def one(v):
            for h in range(2):
                blocks = swap_blocks([frecv[stage, o, tile(2 * v + h), :] for o in range(OFFS)], lane)
                for k in range(4):
                    far_fine[stage, v, pl.ds(8 * (4 * h + k), 8), :] = blocks[k]
            picked = [lane_pick(packed[2 * v + a // 4], widen[a % 4]) for a in range(8)]
            columns = half_both(HALF, far_a, far_c, picked, v)
            for j in range(8):
                far_coarse[stage, v, pl.ds(j, 8, stride=8), :] = columns[j]

        loop(NVAR, one, UNROLL_EXPAND)

    def mortar_terms(factor):
        def fluxes(i):
            rows = pl.ds(pl.multiple_of(i * 16, 16), 16)
            live = jnp.concatenate([coarse_live, coarse_live], axis=0)
            left = [blend(own_coarse, (v, rows, slice(None)), factor) for v in range(NVAR)]
            right = [blend(far_fine, (v, rows, slice(None)), factor) for v in range(NVAR)]
            mean, jump = face_parts(left, right, 1)
            for v in range(NVAR):
                coarse_term[v, rows, :] = jnp.where(live, mean[v] - jump[v], 0.0)
            live = jnp.concatenate([fine_live, fine_live], axis=0)
            left = [blend(far_coarse, (v, rows, slice(None)), factor) for v in range(NVAR)]
            right = [blend(own_fine, (v, rows, slice(None)), factor) for v in range(NVAR)]
            mean, jump = face_parts(left, right, 1)
            for v in range(NVAR):
                fine_term[v, rows, :] = jnp.where(live, mean[v] + jump[v], 0.0)

        loop(4, fluxes, UNROLL_FACE)

        def scatter(v):
            values = [coarse_term[v, pl.ds(8 * a, 8), :] for a in range(8)]
            columns = half_both(BACK, own_a, own_c, values, v)
            for c in range(8):
                total = columns[c] + pltpu.roll(columns[c], 127, 1)
                total = total + pltpu.roll(total, 126, 1)
                share = jnp.where(c_present, lane_pick(total, c_source), 0.0)
                rate[v, pl.ds(56 + c, 8, stride=64), :] += LIFT * share
            turned = rotated(lambda rows: fine_term[v, rows, :], turns)
            for a in range(8):
                share = jnp.where(f_present, lane_pick(turned[a], f_source), 0.0)
                rate[v, pl.ds(64 * a, 8), :] += LIFT * share

        loop(NVAR, scatter, UNROLL_SCATTER)

    fine_first = fine_copies(0)
    coarse_first = coarse_copies(0)
    send_mortars(read_state, 0, fine_first, coarse_first)
    volume_z(u)
    volume_y(u)
    speed = finish_round(round_1, speed, 0)
    vsend[1, 0:1] = speed
    for copy in round_2:
        copy.start()
    volume_x(u)
    x_faces(u)
    own_interpolated(read_state, 0)
    for copy in z_first:
        copy.wait_recv()
    z_faces(None)
    speed = finish_round(round_2, speed, cuts - 1)
    vsend[2, 0:1] = speed
    for copy in round_3:
        copy.start()
    for copy in fine_first + coarse_first:
        copy.wait_recv()
    expand(0)
    mortar_terms(None)

    z_second = z_copies(1)
    z_traces(read_rate, 1)
    for copy in z_second:
        copy.start()
    fine_second = fine_copies(1)
    coarse_second = coarse_copies(1)
    send_mortars(read_rate, 1, fine_second, coarse_second)
    own_interpolated(read_rate, 1)
    speed = finish_round(round_3, speed, cuts + ys - 2)
    step = 0.005 / jnp.max(speed, axis=1, keepdims=True)
    scale = jnp.broadcast_to(negative[0:1] * step, (32, LANES))
    factor = section_b[0] * step

    def first_update(i):
        rows = pl.ds(pl.multiple_of(i * 32, 32), 32)
        state = []
        for v in range(NVAR):
            change = scale * rate[v, rows, :]
            reg_ref[v, rows, :] = change
            state.append(u[v, rows, :] + section_b[0] * change)
            sect[v, rows, :] = state[v]
        inverse, velocity, pressure = primitives(state)
        for d in range(3):
            prim[d, rows, :] = velocity[d]
        prim[3, rows, :] = pressure

    loop(16, first_update, UNROLL_UPDATE)

    volume_z(sect)
    volume_y(sect)
    volume_x(sect)
    x_faces(sect)
    for copy in z_second:
        copy.wait_recv()
    z_faces(factor)
    for copy in fine_second + coarse_second:
        copy.wait_recv()
    expand(1)
    mortar_terms(factor)

    def second_update(i):
        rows = pl.ds(pl.multiple_of(i * 32, 32), 32)
        for v in range(NVAR):
            register = section_a[1] * reg_ref[v, rows, :] + scale * rate[v, rows, :]
            reg_ref[v, rows, :] = register
            adv_ref[v, rows, :] = sect[v, rows, :] + section_b[1] * register

    loop(16, second_update, UNROLL_UPDATE)
    for copies in (round_1, round_2, round_3, z_first, z_second, fine_first, fine_second, coarse_first, coarse_second):
        for copy in copies:
            copy.wait_send()


def on_device(
    slabs, cuts, ys, zs,
    conserved,
    refinement,
    x_neighbour,
    coarse_element,
    quadrant,
    send_count,
    fine_element,
    orientation,
    receive_count,
):
    peers = cuts + ys + zs - 3
    state = (NVAR, NP * FACE, LANES)
    face = (NVAR, FACE, LANES)
    links = (OFFS, CAP)
    tables = (
        refinement.reshape(1, LANES), x_neighbour, coarse_element.reshape(links),
        quadrant.reshape(links), fine_element.reshape(links), orientation.reshape(links),
        send_count.reshape(1, OFFS), receive_count.reshape(1, OFFS),
    )
    ints = jnp.zeros((64, LANES), jnp.int32)
    for i, table in enumerate(tables):
        rows, columns = table.shape
        ints = jnp.maximum(ints, jnp.pad(table, ((8 * i, 64 - 8 * i - rows), (0, LANES - columns))))
    return pl.pallas_call(
        functools.partial(kernel, slabs, cuts, ys, zs),
        out_shape=[jax.ShapeDtypeStruct(state, jnp.float32)] * 2,
        in_specs=[pl.BlockSpec(memory_space=pltpu.HBM), pl.BlockSpec(memory_space=pltpu.VMEM)],
        out_specs=[pl.BlockSpec(memory_space=pltpu.VMEM)] * 2,
        scratch_shapes=[
            pltpu.VMEM(state, jnp.float32),
            pltpu.VMEM((4, NP * FACE, LANES), jnp.float32),
            pltpu.VMEM(state, jnp.float32),
            pltpu.VMEM(state, jnp.float32),
            pltpu.VMEM((2, 2) + face, jnp.float32),
            pltpu.VMEM((2, 2) + face, jnp.float32),
            pltpu.VMEM((2, OFFS, 24, LANES), jnp.float32),
            pltpu.VMEM((2, OFFS, 24, LANES), jnp.float32),
            pltpu.VMEM((2, OFFS, 80, LANES), jnp.float32),
            pltpu.VMEM((2, OFFS, 80, LANES), jnp.float32),
            pltpu.VMEM((3, 8, LANES), jnp.float32),
            pltpu.VMEM((peers, 8, LANES), jnp.float32),
            pltpu.VMEM((2,) + face, jnp.float32),
            pltpu.VMEM((2,) + face, jnp.float32),
            pltpu.VMEM((2,) + face, jnp.float32),
            pltpu.VMEM((2,) + face, jnp.float32),
            pltpu.VMEM(face, jnp.float32),
            pltpu.VMEM(face, jnp.float32),
            pltpu.VMEM(face, jnp.float32),
            pltpu.VMEM((12, 8, LANES), jnp.float32),
            pltpu.SemaphoreType.DMA((8,)),
            pltpu.SemaphoreType.DMA((2, 2)),
            pltpu.SemaphoreType.DMA((2, 2)),
            pltpu.SemaphoreType.DMA((2, OFFS)),
            pltpu.SemaphoreType.DMA((2, OFFS)),
            pltpu.SemaphoreType.DMA((2, OFFS)),
            pltpu.SemaphoreType.DMA((2, OFFS)),
            pltpu.SemaphoreType.DMA((peers,)),
            pltpu.SemaphoreType.DMA((peers,)),
        ],
        compiler_params=pltpu.CompilerParams(
            collective_id=0, has_side_effects=True, vmem_limit_bytes=51 * 1024 * 1024
        ),
    )(conserved, ints)


def solution(mesh):
    slabs, cuts = mesh.shape["slab"], mesh.shape["cut"]
    zs = 12 if slabs % 12 == 0 else 3
    return jax.shard_map(
        functools.partial(on_device, slabs, cuts, slabs // zs, zs),
        mesh=mesh,
        in_specs=(
            P(None, None, ("slab", "cut")),
            P(("slab", "cut")),
            P(("slab", "cut"), None),
            P("slab", "cut", None, None),
            P("slab", "cut", None, None),
            P("slab", "cut", None),
            P("slab", "cut", None, None),
            P("slab", "cut", None, None),
            P("slab", "cut", None),
        ),
        out_specs=(P(None, None, ("slab", "cut")), P(None, None, ("slab", "cut"))),
        check_vma=False,
    )
```

```python
import functools

import jax
import jax.numpy as jnp
import numpy as np
from jax import lax
from jax.experimental import pallas as pl
from jax.experimental.pallas import tpu as pltpu
from jax.sharding import PartitionSpec as P

NP = 8
NVAR = 5
FACE = NP * NP
LANES = 128
OFFS = 4
CAP = 32
UNROLL_SEND = NVAR
UNROLL_OWN = NVAR
UNROLL_EXPAND = 1
UNROLL_SCATTER = NVAR
UNROLL_FACE = 4
UNROLL_VOLUME = 2
UNROLL_UPDATE = 4
MESH = pl.DeviceIdType.MESH

section_a = (0.0, -567301805773.0 / 1357537059087.0)
section_b = (1432997174477.0 / 9575080441755.0, 5161836677717.0 / 13612068292357.0)


def legendre_rows(points, node_count):
    legendre = np.zeros((node_count, node_count))
    legendre[:, 0] = 1.0
    legendre[:, 1] = points
    for degree in range(2, node_count):
        legendre[:, degree] = (
            (2 * degree - 1) * points * legendre[:, degree - 1]
            - (degree - 1) * legendre[:, degree - 2]
        ) / degree
    return legendre


def lobatto(node_count):
    poly_order = node_count - 1
    points = -np.cos(np.pi * np.arange(node_count) / poly_order)
    for newton_step in range(40):
        legendre = legendre_rows(points, node_count)
        points = points - (points * legendre[:, poly_order] - legendre[:, poly_order - 1]) / (
            node_count * legendre[:, poly_order]
        )
    top_row = legendre_rows(points, node_count)[:, poly_order]
    weights = 2.0 / (poly_order * node_count * top_row * top_row)
    differ = np.zeros((node_count, node_count))
    for target in range(node_count):
        for source in range(node_count):
            if target != source:
                differ[target, source] = top_row[target] / (
                    top_row[source] * (points[target] - points[source])
                )
    differ[0, 0] = -poly_order * node_count / 4.0
    differ[poly_order, poly_order] = poly_order * node_count / 4.0
    lower_half = np.zeros((node_count, node_count))
    targets = (points - 1) / 2.0
    for source in range(node_count):
        basis = np.ones(node_count)
        for other in range(node_count):
            if other != source:
                basis = basis * (targets - points[other]) / (points[source] - points[other])
        lower_half[:, source] = basis
    lower_back = 0.5 * np.transpose(lower_half) * weights[None, :] / weights[:, None]
    return (weights, differ, lower_half, lower_back)


WEIGHTS, DIFFER, HALF, BACK = lobatto(NP)
LIFT = float(1.0 / WEIGHTS[0])
EVEN = 0.5 * (DIFFER[:4, :4] + DIFFER[:4, :3:-1])
ODD = 0.5 * (DIFFER[:4, :4] - DIFFER[:4, :3:-1])


def combine(row, values):
    total = None
    for weight, value in zip(row, values):
        weight = float(np.float32(weight))
        if abs(weight) < 1e-12:
            continue
        term = value if weight == 1.0 else weight * value
        total = term if total is None else total + term
    return total


def derive(f):
    even = [f[j] + f[7 - j] for j in range(4)]
    odd = [f[j] - f[7 - j] for j in range(4)]
    out = [None] * 8
    for i in range(4):
        from_even = combine(EVEN[i], even)
        from_odd = combine(ODD[i], odd)
        out[i] = from_odd + from_even
        out[7 - i] = from_odd - from_even
    return out


def half_map(matrix, upper, f):
    f = [jnp.where(upper, f[7 - j], f[j]) for j in range(8)]
    g = [combine(matrix[i], f) for i in range(8)]
    return [jnp.where(upper, g[7 - i], g[i]) for i in range(8)]


def primitives(u):
    inverse = 1.0 / u[0]
    velocity = [u[1] * inverse, u[2] * inverse, u[3] * inverse]
    carried = u[1] * velocity[0] + u[2] * velocity[1] + u[3] * velocity[2]
    pressure = 0.4 * (u[4] - 0.5 * carried)
    return inverse, velocity, pressure


def flux_of(u, normal, pressure, direction):
    rows = [u[1 + direction]]
    for column in range(3):
        carried = u[1 + column] * normal
        rows.append(carried + pressure if column == direction else carried)
    rows.append(normal * (u[4] + pressure))
    return rows


def face_flux(u, direction):
    inverse, velocity, pressure = primitives(u)
    normal = velocity[direction]
    speed = jnp.abs(normal) + jnp.sqrt(1.4 * pressure * inverse)
    return flux_of(u, normal, pressure, direction), speed


def face_parts(left, right, direction):
    left_flux, left_speed = face_flux(left, direction)
    right_flux, right_speed = face_flux(right, direction)
    half_speed = 0.5 * jnp.maximum(left_speed, right_speed)
    mean = [0.5 * (r - l) for l, r in zip(left_flux, right_flux)]
    jump = [half_speed * (r - l) for l, r in zip(left, right)]
    return mean, jump


def lane_pick(x, index):
    return jnp.take_along_axis(x, index, axis=1, mode="promise_in_bounds")


def swap_blocks(x, lane):
    high = lane >= 64
    odd = (lane // 32) % 2 == 1
    y = list(x)
    for k in (0, 1):
        y[k] = jnp.where(high, pltpu.roll(x[k + 2], 64, 1), x[k])
        y[k + 2] = jnp.where(high, x[k + 2], pltpu.roll(x[k], 64, 1))
    z = list(y)
    for k in (0, 2):
        z[k] = jnp.where(odd, pltpu.roll(y[k + 1], 32, 1), y[k])
        z[k + 1] = jnp.where(odd, y[k + 1], pltpu.roll(y[k], 96, 1))
    return z


def offset_distance(offset_index):
    return (offset_index // 2 + 1) * (1 - 2 * (offset_index % 2))


def eight(row):
    return jnp.broadcast_to(row, (8, LANES))


def tile(i):
    return pl.ds(pl.multiple_of(i * 8, 8), 8)


def loop(count, body, unroll):
    def step(i, carry):
        body(i)
        return carry

    lax.fori_loop(0, count, step, 0, unroll=unroll)


def kernel(
    slabs, cuts, ys, zs,
    u_hbm, ints_ref,
    rate, reg_ref, sect, scale_ref,
    u,
    prim,
    zsend, zrecv, csend, crecv, fsend, frecv,
    vsend, vrecv,
    own_coarse, own_fine, far_coarse, far_fine, coarse_term, fine_term, work, packed,
    in_sem, zs_sem, zr_sem, cs_sem, cr_sem, fs_sem, fr_sem, vs_sem, vr_sem,
):
    s = lax.axis_index("slab")
    t = lax.axis_index("cut")
    y = s // zs
    z = s % zs
    cut_peers = [(s, (t + d) % cuts) for d in range(1, cuts)]
    y_peers = [(((y + d) % ys) * zs + z, t) for d in range(1, ys)]
    z_peers = [(y * zs + (z + d) % zs, t) for d in range(1, zs)]
    ahead = [((s + offset_distance(o) + slabs) % slabs, t) for o in range(OFFS)]
    back = [((s - offset_distance(o) + slabs) % slabs, t) for o in range(OFFS)]

    loads = [
        pltpu.make_async_copy(
            u_hbm.at[:, pl.ds(64 * a, 64), :], u.at[:, pl.ds(64 * a, 64), :], in_sem.at[a]
        )
        for a in range(8)
    ]
    for copy in loads:
        copy.start()

    barrier = pltpu.get_barrier_semaphore()
    greeted = cut_peers + y_peers + z_peers + ahead
    for peer in greeted:
        pl.semaphore_signal(barrier, inc=1, device_id=peer, device_id_type=MESH)

    lane = lax.broadcasted_iota(jnp.int32, (8, LANES), 1)
    sub = lax.broadcasted_iota(jnp.int32, (8, LANES), 0)
    flipped = 7 - sub
    block = lane // CAP
    spread = lax.broadcasted_iota(jnp.int32, (LANES, LANES), 0)
    counting = (lane + 1).astype(jnp.float32)

    level = eight(ints_ref[0:1])
    metric = jnp.where(level == 0, 1.0, jnp.where(level == 1, 2.0, 4.0))
    negative = -metric

    fastest = jnp.zeros((32, LANES), jnp.float32)
    for a in range(8):
        loads[a].wait()

        def one(i, fastest):
            rows = pl.ds(pl.multiple_of(64 * a + i * 32, 32), 32)
            state = [u[v, rows, :] for v in range(NVAR)]
            inverse, velocity, pressure = primitives(state)
            for d in range(3):
                prim[d, rows, :] = velocity[d]
            prim[3, rows, :] = pressure
            square = velocity[0] * velocity[0] + velocity[1] * velocity[1] + velocity[2] * velocity[2]
            return jnp.maximum(fastest, jnp.sqrt(square) + jnp.sqrt(1.4 * pressure * inverse))

        fastest = lax.fori_loop(0, 2, one, fastest, unroll=True)
    speed = jnp.maximum(jnp.maximum(fastest[0:8], fastest[8:16]), jnp.maximum(fastest[16:24], fastest[24:32]))
    speed = jnp.max(speed * metric, axis=0, keepdims=True)
    vsend[0, 0:1] = speed

    def speed_round(number, first, peers):
        return [
            pltpu.make_async_remote_copy(
                src_ref=vsend.at[number, pl.ds(0, 1)], dst_ref=vrecv.at[first + i, pl.ds(0, 1)],
                send_sem=vs_sem.at[first + i], recv_sem=vr_sem.at[first + i],
                device_id=peer, device_id_type=MESH)
            for i, peer in enumerate(peers)
        ]

    def finish_round(copies, value, first):
        for copy in copies:
            copy.wait_recv()
        for i in range(len(copies)):
            value = jnp.maximum(value, vrecv[first + i, 0:1])
        return value

    round_1 = speed_round(0, 0, cut_peers)
    round_2 = speed_round(1, cuts - 1, y_peers)
    round_3 = speed_round(2, cuts + ys - 2, z_peers)

    def z_copies(stage):
        targets = [(s, (t + 1) % cuts), (s, (t + cuts - 1) % cuts)]
        return [
            pltpu.make_async_remote_copy(
                src_ref=zsend.at[stage, i], dst_ref=zrecv.at[stage, i],
                send_sem=zs_sem.at[stage, i], recv_sem=zr_sem.at[stage, i],
                device_id=targets[i], device_id_type=MESH)
            for i in range(2)
        ]

    def fine_copies(stage):
        return [
            pltpu.make_async_remote_copy(
                src_ref=fsend.at[stage, o], dst_ref=frecv.at[stage, o],
                send_sem=fs_sem.at[stage, o], recv_sem=fr_sem.at[stage, o],
                device_id=back[o], device_id_type=MESH)
            for o in (2, 3, 0, 1)
        ]

    def coarse_copies(stage):
        return [
            pltpu.make_async_remote_copy(
                src_ref=csend.at[stage, o], dst_ref=crecv.at[stage, o],
                send_sem=cs_sem.at[stage, o], recv_sem=cr_sem.at[stage, o],
                device_id=ahead[o], device_id_type=MESH)
            for o in (2, 3, 0, 1)
        ]

    pl.semaphore_wait(barrier, len(greeted))
    for copy in round_1:
        copy.start()

    def z_traces(read, stage):
        for v in range(NVAR):
            zsend[stage, 0, v] = read(v, pl.ds(7, FACE, stride=8))
            zsend[stage, 1, v] = read(v, pl.ds(0, FACE, stride=8))

    def read_state(v, rows):
        return u[v, rows, :]

    def read_rate(v, rows):
        values = rate[v, rows, :]
        return jnp.broadcast_to(negative[0:1], values.shape) * values

    def row_of(first):
        parts = [ints_ref[first + o : first + o + 1, 0:CAP] for o in range(OFFS)]
        return eight(jnp.concatenate(parts, axis=1))

    def live_of(row):
        count = jnp.broadcast_to(ints_ref[row : row + 1, 0:1], (8, LANES))
        for o in range(1, OFFS):
            count = jnp.where(block == o, jnp.broadcast_to(ints_ref[row : row + 1, o : o + 1], (8, LANES)), count)
        return lane % CAP < count

    neighbour = eight(ints_ref[8:9])
    coarse_index = row_of(16)
    quadrant = row_of(24)
    fine_index = row_of(32)
    turns = row_of(40)
    coarse_live = live_of(48)
    fine_live = live_of(56)
    own_a = quadrant >= 2
    own_c = quadrant % 2 == 1
    back_turns = (4 - turns) % 4
    group_pick = block * CAP + (lane % 8) * 4
    group_index = lane_pick(coarse_index, group_pick)
    group_block = (lane // 8) % 4
    widen = [block * CAP + k * 8 + (lane % CAP) // 4 for k in range(4)]

    def rev(x):
        return jnp.take_along_axis(x, flipped, axis=0, mode="promise_in_bounds")

    def rotated(read, amount):
        odd = amount % 2 == 1
        far = amount >= 2
        mixed = [
            jnp.where(odd, read(pl.ds(7 - i, 8, stride=8)), read(pl.ds(8 * i, 8)))
            for i in range(8)
        ]
        return [jnp.where(far, rev(mixed[7 - i]), mixed[i]) for i in range(8)]

    def half_both(matrix, upper_a, upper_c, values, v):
        along_a = half_map(matrix, upper_a, values)
        for i in range(8):
            work[v, pl.ds(8 * i, 8), :] = along_a[i]
        columns = [work[v, pl.ds(j, 8, stride=8), :] for j in range(8)]
        return half_map(matrix, upper_c, columns)

    def send_mortars(read, stage, fine, coarse):
        def fine_side(v):
            for a in range(8):
                work[v, pl.ds(8 * a, 8), :] = lane_pick(read(v, pl.ds(64 * a, 8)), fine_index)
            turned = rotated(lambda rows: work[v, rows, :], back_turns)
            for a in range(8):
                own_fine[stage, v, pl.ds(8 * a, 8), :] = turned[a]
            for h in range(2):
                blocks = swap_blocks(turned[4 * h : 4 * h + 4], lane)
                for o in range(OFFS):
                    fsend[stage, o, tile(2 * v + h), :] = blocks[o]

        loop(NVAR, fine_side, UNROLL_SEND)
        for copy in fine:
            copy.start()

        def coarse_side(v):
            for h in range(2):
                pack = lane_pick(read(v, pl.ds(256 * h + 56, 8)), group_index)
                for k in range(1, 4):
                    top = read(v, pl.ds(256 * h + 64 * k + 56, 8))
                    pack = jnp.where(group_block == k, lane_pick(top, group_index), pack)
                packed[2 * v + h] = pack

        loop(NVAR, coarse_side, UNROLL_SEND)
        packed[10] = quadrant.astype(jnp.float32)
        packed[11] = jnp.zeros((8, LANES), jnp.float32)
        for m in range(3):
            blocks = swap_blocks([packed[4 * m + k] for k in range(4)], lane)
            for o in range(OFFS):
                csend[stage, o, pl.ds(8 * m, 8), :] = blocks[o]
        for copy in coarse:
            copy.start()

    def own_interpolated(read, stage):
        def one(v):
            picked = [lane_pick(read(v, pl.ds(64 * a + 56, 8)), coarse_index) for a in range(8)]
            columns = half_both(HALF, own_a, own_c, picked, v)
            for j in range(8):
                own_coarse[stage, v, pl.ds(j, 8, stride=8), :] = columns[j]

        loop(NVAR, one, UNROLL_OWN)

    def line(read, normal, pressure, direction, v):
        if v == 0:
            return [read(1 + direction, j) for j in range(8)]
        if v == 4:
            return [normal[j] * (read(4, j) + pressure[j]) for j in range(8)]
        if v == 1 + direction:
            return [read(v, j) * normal[j] + pressure[j] for j in range(8)]
        return [read(v, j) * normal[j] for j in range(8)]

    def volume(state, direction, at, fresh):
        def one(i):
            normal = [prim[direction, at(i, j), :] for j in range(8)]
            pressure = [prim[3, at(i, j), :] for j in range(8)]
            for v in range(NVAR):
                out = derive(line(lambda w, j: state[w, at(i, j), :], normal, pressure, direction, v))
                for j in range(8):
                    if fresh:
                        rate[v, at(i, j), :] = out[j]
                    else:
                        rate[v, at(i, j), :] += out[j]

        loop(8, one, UNROLL_VOLUME)

    def volume_z(state):
        volume(state, 2, lambda a, j: pl.ds(a * 64 + j, 8, stride=8), True)

    def volume_y(state):
        volume(state, 1, lambda a, j: pl.ds(pl.multiple_of(a * 64 + j * 8, 8), 8), False)

    def volume_x(state):
        volume(state, 0, lambda b, j: pl.ds(pl.multiple_of(b * 8 + j * 64, 8), 8), False)

    def inverse_of(row, counts):
        table = jnp.where(spread == row, 1.0, 0.0).astype(jnp.bfloat16)
        found = lax.dot_general(
            counts.astype(jnp.bfloat16), table, (((1,), (1,)), ((), ())),
            preferred_element_type=jnp.float32,
        )
        present = found > 0.5
        return jnp.maximum(found - 1.0, 0.0).astype(jnp.int32), present

    x_source, _ = inverse_of(neighbour[0:1], counting)
    c_source, c_present = inverse_of(coarse_index[0:1], jnp.where(lane % 4 == 0, counting, 0.0))
    f_source, f_present = inverse_of(fine_index[0:1], counting)

    def x_faces(state):
        def one(i):
            low = pl.ds(pl.multiple_of(i * 16, 16), 16)
            high = pl.ds(pl.multiple_of(448 + i * 16, 16), 16)
            pick = jnp.broadcast_to(neighbour[0:1], (16, LANES))
            source = jnp.broadcast_to(x_source[0:1], (16, LANES))
            left = [state[v, high, :] for v in range(NVAR)]
            right = [lane_pick(state[v, low, :], pick) for v in range(NVAR)]
            mean, jump = face_parts(left, right, 0)
            for v in range(NVAR):
                rate[v, high, :] += LIFT * (mean[v] - jump[v])
                rate[v, low, :] += LIFT * lane_pick(mean[v] + jump[v], source)

        loop(4, one, UNROLL_FACE)

    def blend(ref, index, factor):
        if factor is None:
            return ref[(0,) + index]
        first = ref[(0,) + index]
        return first + jnp.broadcast_to(factor, first.shape) * ref[(1,) + index]

    def z_faces(factor):
        def one(i):
            rows = pl.ds(pl.multiple_of(i * 16, 16), 16)
            bottom = pl.ds(i * 128, 16, stride=8)
            top = pl.ds(i * 128 + 7, 16, stride=8)
            left = [blend(zsend, (0, v, rows, slice(None)), factor) for v in range(NVAR)]
            right = [blend(zrecv, (1, v, rows, slice(None)), factor) for v in range(NVAR)]
            mean, jump = face_parts(left, right, 2)
            for v in range(NVAR):
                rate[v, top, :] += LIFT * (mean[v] - jump[v])
            left = [blend(zrecv, (0, v, rows, slice(None)), factor) for v in range(NVAR)]
            right = [blend(zsend, (1, v, rows, slice(None)), factor) for v in range(NVAR)]
            mean, jump = face_parts(left, right, 2)
            for v in range(NVAR):
                rate[v, bottom, :] += LIFT * (mean[v] + jump[v])

        loop(4, one, UNROLL_FACE)

    def far_quadrants():
        far = packed[10]
        return far > 1.5, (far == 1.0) | (far == 3.0)

    def expand(stage):
        for m in range(3):
            blocks = swap_blocks([crecv[stage, o, pl.ds(8 * m, 8), :] for o in range(OFFS)], lane)
            for k in range(4):
                packed[4 * m + k] = blocks[k]
        far_a, far_c = far_quadrants()

        def one(v):
            for h in range(2):
                blocks = swap_blocks([frecv[stage, o, tile(2 * v + h), :] for o in range(OFFS)], lane)
                for k in range(4):
                    far_fine[stage, v, pl.ds(8 * (4 * h + k), 8), :] = blocks[k]
            picked = [lane_pick(packed[2 * v + a // 4], widen[a % 4]) for a in range(8)]
            columns = half_both(HALF, far_a, far_c, picked, v)
            for j in range(8):
                far_coarse[stage, v, pl.ds(j, 8, stride=8), :] = columns[j]

        loop(NVAR, one, UNROLL_EXPAND)

    def mortar_terms(factor):
        def fluxes(i):
            rows = pl.ds(pl.multiple_of(i * 16, 16), 16)
            live = jnp.concatenate([coarse_live, coarse_live], axis=0)
            left = [blend(own_coarse, (v, rows, slice(None)), factor) for v in range(NVAR)]
            right = [blend(far_fine, (v, rows, slice(None)), factor) for v in range(NVAR)]
            mean, jump = face_parts(left, right, 1)
            for v in range(NVAR):
                coarse_term[v, rows, :] = jnp.where(live, mean[v] - jump[v], 0.0)
            live = jnp.concatenate([fine_live, fine_live], axis=0)
            left = [blend(far_coarse, (v, rows, slice(None)), factor) for v in range(NVAR)]
            right = [blend(own_fine, (v, rows, slice(None)), factor) for v in range(NVAR)]
            mean, jump = face_parts(left, right, 1)
            for v in range(NVAR):
                fine_term[v, rows, :] = jnp.where(live, mean[v] + jump[v], 0.0)

        loop(4, fluxes, UNROLL_FACE)

        def scatter(v):
            values = [coarse_term[v, pl.ds(8 * a, 8), :] for a in range(8)]
            columns = half_both(BACK, own_a, own_c, values, v)
            for c in range(8):
                total = columns[c] + pltpu.roll(columns[c], 127, 1)
                total = total + pltpu.roll(total, 126, 1)
                share = jnp.where(c_present, lane_pick(total, c_source), 0.0)
                rate[v, pl.ds(56 + c, 8, stride=64), :] += LIFT * share
            turned = rotated(lambda rows: fine_term[v, rows, :], turns)
            for a in range(8):
                share = jnp.where(f_present, lane_pick(turned[a], f_source), 0.0)
                rate[v, pl.ds(64 * a, 8), :] += LIFT * share

        loop(NVAR, scatter, UNROLL_SCATTER)

    fine_first = fine_copies(0)
    coarse_first = coarse_copies(0)
    send_mortars(read_state, 0, fine_first, coarse_first)
    z_first = z_copies(0)
    z_traces(read_state, 0)
    for copy in z_first:
        copy.start()
    volume_z(u)
    volume_y(u)
    speed = finish_round(round_1, speed, 0)
    vsend[1, 0:1] = speed
    for copy in round_2:
        copy.start()
    volume_x(u)
    x_faces(u)
    own_interpolated(read_state, 0)
    speed = finish_round(round_2, speed, cuts - 1)
    vsend[2, 0:1] = speed
    for copy in round_3:
        copy.start()
    for copy in fine_first + coarse_first:
        copy.wait_recv()
    expand(0)
    mortar_terms(None)
    for copy in z_first:
        copy.wait_recv()
    z_faces(None)

    fine_second = fine_copies(1)
    coarse_second = coarse_copies(1)
    send_mortars(read_rate, 1, fine_second, coarse_second)
    z_second = z_copies(1)
    z_traces(read_rate, 1)
    for copy in z_second:
        copy.start()
    own_interpolated(read_rate, 1)
    speed = finish_round(round_3, speed, cuts + ys - 2)
    step = 0.005 / jnp.max(speed, axis=1, keepdims=True)
    scale = jnp.broadcast_to(negative[0:1] * step, (32, LANES))
    factor = section_b[0] * step
    scale_ref[...] = scale[0:8]

    def first_update(i):
        rows = pl.ds(pl.multiple_of(i * 32, 32), 32)
        state = []
        for v in range(NVAR):
            change = scale * rate[v, rows, :]
            reg_ref[v, rows, :] = section_a[1] * change
            state.append(u[v, rows, :] + section_b[0] * change)
            sect[v, rows, :] = state[v]
        inverse, velocity, pressure = primitives(state)
        for d in range(3):
            prim[d, rows, :] = velocity[d]
        prim[3, rows, :] = pressure

    loop(16, first_update, UNROLL_UPDATE)

    volume_z(sect)
    volume_y(sect)
    volume_x(sect)
    x_faces(sect)
    for copy in fine_second + coarse_second:
        copy.wait_recv()
    expand(1)
    mortar_terms(factor)
    for copy in z_second:
        copy.wait_recv()
    z_faces(factor)

    for copies in (round_1, round_2, round_3, z_first, z_second, fine_first, fine_second, coarse_first, coarse_second):
        for copy in copies:
            copy.wait_send()


def on_device(
    slabs, cuts, ys, zs,
    conserved,
    refinement,
    x_neighbour,
    coarse_element,
    quadrant,
    send_count,
    fine_element,
    orientation,
    receive_count,
):
    peers = cuts + ys + zs - 3
    state = (NVAR, NP * FACE, LANES)
    face = (NVAR, FACE, LANES)
    links = (OFFS, CAP)
    tables = (
        refinement.reshape(1, LANES), x_neighbour, coarse_element.reshape(links),
        quadrant.reshape(links), fine_element.reshape(links), orientation.reshape(links),
        send_count.reshape(1, OFFS), receive_count.reshape(1, OFFS),
    )
    ints = jnp.zeros((64, LANES), jnp.int32)
    for i, table in enumerate(tables):
        rows, columns = table.shape
        ints = jnp.maximum(ints, jnp.pad(table, ((8 * i, 64 - 8 * i - rows), (0, LANES - columns))))
    rate, before, sectioned, scale = pl.pallas_call(
        functools.partial(kernel, slabs, cuts, ys, zs),
        out_shape=[jax.ShapeDtypeStruct(state, jnp.float32)] * 3
        + [jax.ShapeDtypeStruct((8, LANES), jnp.float32)],
        in_specs=[pl.BlockSpec(memory_space=pltpu.HBM), pl.BlockSpec(memory_space=pltpu.VMEM)],
        out_specs=[pl.BlockSpec(memory_space=pltpu.VMEM)] * 4,
        scratch_shapes=[
            pltpu.VMEM(state, jnp.float32),
            pltpu.VMEM((4, NP * FACE, LANES), jnp.float32),
            pltpu.VMEM((2, 2) + face, jnp.float32),
            pltpu.VMEM((2, 2) + face, jnp.float32),
            pltpu.VMEM((2, OFFS, 24, LANES), jnp.float32),
            pltpu.VMEM((2, OFFS, 24, LANES), jnp.float32),
            pltpu.VMEM((2, OFFS, 80, LANES), jnp.float32),
            pltpu.VMEM((2, OFFS, 80, LANES), jnp.float32),
            pltpu.VMEM((3, 8, LANES), jnp.float32),
            pltpu.VMEM((peers, 8, LANES), jnp.float32),
            pltpu.VMEM((2,) + face, jnp.float32),
            pltpu.VMEM((2,) + face, jnp.float32),
            pltpu.VMEM((2,) + face, jnp.float32),
            pltpu.VMEM((2,) + face, jnp.float32),
            pltpu.VMEM(face, jnp.float32),
            pltpu.VMEM(face, jnp.float32),
            pltpu.VMEM(face, jnp.float32),
            pltpu.VMEM((12, 8, LANES), jnp.float32),
            pltpu.SemaphoreType.DMA((8,)),
            pltpu.SemaphoreType.DMA((2, 2)),
            pltpu.SemaphoreType.DMA((2, 2)),
            pltpu.SemaphoreType.DMA((2, OFFS)),
            pltpu.SemaphoreType.DMA((2, OFFS)),
            pltpu.SemaphoreType.DMA((2, OFFS)),
            pltpu.SemaphoreType.DMA((2, OFFS)),
            pltpu.SemaphoreType.DMA((peers,)),
            pltpu.SemaphoreType.DMA((peers,)),
        ],
        compiler_params=pltpu.CompilerParams(
            collective_id=0, has_side_effects=True, vmem_limit_bytes=50 * 1024 * 1024
        ),
    )(conserved, ints)
    register = before + scale[0] * rate
    return sectioned + section_b[1] * register, register


def solution(mesh):
    slabs, cuts = mesh.shape["slab"], mesh.shape["cut"]
    zs = 12 if slabs % 12 == 0 else 3
    return jax.shard_map(
        functools.partial(on_device, slabs, cuts, slabs // zs, zs),
        mesh=mesh,
        in_specs=(
            P(None, None, ("slab", "cut")),
            P(("slab", "cut")),
            P(("slab", "cut"), None),
            P("slab", "cut", None, None),
            P("slab", "cut", None, None),
            P("slab", "cut", None),
            P("slab", "cut", None, None),
            P("slab", "cut", None, None),
            P("slab", "cut", None),
        ),
        out_specs=(P(None, None, ("slab", "cut")), P(None, None, ("slab", "cut"))),
        check_vma=False,
    )
```

```python
import functools

import jax
import jax.numpy as jnp
import numpy as np
from jax import lax
from jax.experimental import pallas as pl
from jax.experimental.pallas import tpu as pltpu
from jax.sharding import PartitionSpec as P

NP = 8
NVAR = 5
FACE = NP * NP
LANES = 128
OFFS = 4
CAP = 32
UNROLL_SEND = NVAR
UNROLL_OWN = NVAR
UNROLL_EXPAND = 1
UNROLL_SCATTER = NVAR
UNROLL_FACE = 4
UNROLL_VOLUME = 2
UNROLL_UPDATE = 4
MESH = pl.DeviceIdType.MESH

section_a = (0.0, -567301805773.0 / 1357537059087.0)
section_b = (1432997174477.0 / 9575080441755.0, 5161836677717.0 / 13612068292357.0)


def legendre_rows(points, node_count):
    legendre = np.zeros((node_count, node_count))
    legendre[:, 0] = 1.0
    legendre[:, 1] = points
    for degree in range(2, node_count):
        legendre[:, degree] = (
            (2 * degree - 1) * points * legendre[:, degree - 1]
            - (degree - 1) * legendre[:, degree - 2]
        ) / degree
    return legendre


def lobatto(node_count):
    poly_order = node_count - 1
    points = -np.cos(np.pi * np.arange(node_count) / poly_order)
    for newton_step in range(40):
        legendre = legendre_rows(points, node_count)
        points = points - (points * legendre[:, poly_order] - legendre[:, poly_order - 1]) / (
            node_count * legendre[:, poly_order]
        )
    top_row = legendre_rows(points, node_count)[:, poly_order]
    weights = 2.0 / (poly_order * node_count * top_row * top_row)
    differ = np.zeros((node_count, node_count))
    for target in range(node_count):
        for source in range(node_count):
            if target != source:
                differ[target, source] = top_row[target] / (
                    top_row[source] * (points[target] - points[source])
                )
    differ[0, 0] = -poly_order * node_count / 4.0
    differ[poly_order, poly_order] = poly_order * node_count / 4.0
    lower_half = np.zeros((node_count, node_count))
    targets = (points - 1) / 2.0
    for source in range(node_count):
        basis = np.ones(node_count)
        for other in range(node_count):
            if other != source:
                basis = basis * (targets - points[other]) / (points[source] - points[other])
        lower_half[:, source] = basis
    lower_back = 0.5 * np.transpose(lower_half) * weights[None, :] / weights[:, None]
    return (weights, differ, lower_half, lower_back)


WEIGHTS, DIFFER, HALF, BACK = lobatto(NP)
LIFT = float(1.0 / WEIGHTS[0])
EVEN = 0.5 * (DIFFER[:4, :4] + DIFFER[:4, :3:-1])
ODD = 0.5 * (DIFFER[:4, :4] - DIFFER[:4, :3:-1])


def combine(row, values):
    total = None
    for weight, value in zip(row, values):
        weight = float(np.float32(weight))
        if abs(weight) < 1e-12:
            continue
        term = value if weight == 1.0 else weight * value
        total = term if total is None else total + term
    return total


def derive(f):
    even = [f[j] + f[7 - j] for j in range(4)]
    odd = [f[j] - f[7 - j] for j in range(4)]
    out = [None] * 8
    for i in range(4):
        from_even = combine(EVEN[i], even)
        from_odd = combine(ODD[i], odd)
        out[i] = from_odd + from_even
        out[7 - i] = from_odd - from_even
    return out


def half_map(matrix, upper, f):
    f = [jnp.where(upper, f[7 - j], f[j]) for j in range(8)]
    g = [combine(matrix[i], f) for i in range(8)]
    return [jnp.where(upper, g[7 - i], g[i]) for i in range(8)]


def primitives(u):
    inverse = 1.0 / u[0]
    velocity = [u[1] * inverse, u[2] * inverse, u[3] * inverse]
    carried = u[1] * velocity[0] + u[2] * velocity[1] + u[3] * velocity[2]
    pressure = 0.4 * (u[4] - 0.5 * carried)
    return inverse, velocity, pressure


def flux_of(u, normal, pressure, direction):
    rows = [u[1 + direction]]
    for column in range(3):
        carried = u[1 + column] * normal
        rows.append(carried + pressure if column == direction else carried)
    rows.append(normal * (u[4] + pressure))
    return rows


def face_flux(u, direction):
    inverse, velocity, pressure = primitives(u)
    normal = velocity[direction]
    speed = jnp.abs(normal) + jnp.sqrt(1.4 * pressure * inverse)
    return flux_of(u, normal, pressure, direction), speed


def face_parts(left, right, direction):
    left_flux, left_speed = face_flux(left, direction)
    right_flux, right_speed = face_flux(right, direction)
    half_speed = 0.5 * jnp.maximum(left_speed, right_speed)
    mean = [0.5 * (r - l) for l, r in zip(left_flux, right_flux)]
    jump = [half_speed * (r - l) for l, r in zip(left, right)]
    return mean, jump


def lane_pick(x, index):
    return jnp.take_along_axis(x, index, axis=1, mode="promise_in_bounds")


def swap_blocks(x, lane):
    high = lane >= 64
    odd = (lane // 32) % 2 == 1
    y = list(x)
    for k in (0, 1):
        y[k] = jnp.where(high, pltpu.roll(x[k + 2], 64, 1), x[k])
        y[k + 2] = jnp.where(high, x[k + 2], pltpu.roll(x[k], 64, 1))
    z = list(y)
    for k in (0, 2):
        z[k] = jnp.where(odd, pltpu.roll(y[k + 1], 32, 1), y[k])
        z[k + 1] = jnp.where(odd, y[k + 1], pltpu.roll(y[k], 96, 1))
    return z


def offset_distance(offset_index):
    return (offset_index // 2 + 1) * (1 - 2 * (offset_index % 2))


def eight(row):
    return jnp.broadcast_to(row, (8, LANES))


def tile(i):
    return pl.ds(pl.multiple_of(i * 8, 8), 8)


def loop(count, body, unroll):
    def step(i, carry):
        body(i)
        return carry

    lax.fori_loop(0, count, step, 0, unroll=unroll)


def kernel(
    slabs, cuts, ys, zs,
    u_hbm, ints_ref,
    rate_1, rate_2, sect, scale_ref,
    u,
    prim, density_1, density_2,
    zsend, zrecv, csend, crecv, fsend, frecv,
    vsend, vrecv,
    own_coarse, own_fine, far_coarse, far_fine, coarse_term, fine_term, work, packed,
    in_sem, zs_sem, zr_sem, cs_sem, cr_sem, fs_sem, fr_sem, vs_sem, vr_sem,
):
    s = lax.axis_index("slab")
    t = lax.axis_index("cut")
    y = s // zs
    z = s % zs
    cut_peers = [(s, (t + d) % cuts) for d in range(1, cuts)]
    y_peers = [(((y + d) % ys) * zs + z, t) for d in range(1, ys)]
    z_peers = [(y * zs + (z + d) % zs, t) for d in range(1, zs)]
    ahead = [((s + offset_distance(o) + slabs) % slabs, t) for o in range(OFFS)]
    back = [((s - offset_distance(o) + slabs) % slabs, t) for o in range(OFFS)]

    loads = [
        pltpu.make_async_copy(
            u_hbm.at[:, pl.ds(64 * a, 64), :], u.at[:, pl.ds(64 * a, 64), :], in_sem.at[a]
        )
        for a in range(8)
    ]
    for copy in loads:
        copy.start()

    barrier = pltpu.get_barrier_semaphore()
    greeted = cut_peers + y_peers + z_peers + ahead
    for peer in greeted:
        pl.semaphore_signal(barrier, inc=1, device_id=peer, device_id_type=MESH)

    lane = lax.broadcasted_iota(jnp.int32, (8, LANES), 1)
    sub = lax.broadcasted_iota(jnp.int32, (8, LANES), 0)
    flipped = 7 - sub
    block = lane // CAP
    spread = lax.broadcasted_iota(jnp.int32, (LANES, LANES), 0)
    counting = (lane + 1).astype(jnp.float32)

    level = eight(ints_ref[0:1])
    metric = jnp.where(level == 0, 1.0, jnp.where(level == 1, 2.0, 4.0))
    negative = -metric

    fastest = jnp.zeros((32, LANES), jnp.float32)
    for a in range(8):
        loads[a].wait()

        def one(i, fastest):
            rows = pl.ds(pl.multiple_of(64 * a + i * 32, 32), 32)
            state = [u[v, rows, :] for v in range(NVAR)]
            inverse, velocity, pressure = primitives(state)
            for d in range(3):
                prim[d, rows, :] = velocity[d]
            prim[3, rows, :] = pressure
            square = velocity[0] * velocity[0] + velocity[1] * velocity[1] + velocity[2] * velocity[2]
            return jnp.maximum(fastest, jnp.sqrt(square) + jnp.sqrt(1.4 * pressure * inverse))

        fastest = lax.fori_loop(0, 2, one, fastest, unroll=True)
    speed = jnp.maximum(jnp.maximum(fastest[0:8], fastest[8:16]), jnp.maximum(fastest[16:24], fastest[24:32]))
    speed = jnp.max(speed * metric, axis=0, keepdims=True)
    vsend[0, 0:1] = speed

    def speed_round(number, first, peers):
        return [
            pltpu.make_async_remote_copy(
                src_ref=vsend.at[number, pl.ds(0, 1)], dst_ref=vrecv.at[first + i, pl.ds(0, 1)],
                send_sem=vs_sem.at[first + i], recv_sem=vr_sem.at[first + i],
                device_id=peer, device_id_type=MESH)
            for i, peer in enumerate(peers)
        ]

    def finish_round(copies, value, first):
        for copy in copies:
            copy.wait_recv()
        for i in range(len(copies)):
            value = jnp.maximum(value, vrecv[first + i, 0:1])
        return value

    round_1 = speed_round(0, 0, cut_peers)
    round_2 = speed_round(1, cuts - 1, y_peers)
    round_3 = speed_round(2, cuts + ys - 2, z_peers)

    def z_copies(stage):
        targets = [(s, (t + 1) % cuts), (s, (t + cuts - 1) % cuts)]
        return [
            pltpu.make_async_remote_copy(
                src_ref=zsend.at[stage, i], dst_ref=zrecv.at[stage, i],
                send_sem=zs_sem.at[stage, i], recv_sem=zr_sem.at[stage, i],
                device_id=targets[i], device_id_type=MESH)
            for i in range(2)
        ]

    def fine_copies(stage):
        return [
            pltpu.make_async_remote_copy(
                src_ref=fsend.at[stage, o], dst_ref=frecv.at[stage, o],
                send_sem=fs_sem.at[stage, o], recv_sem=fr_sem.at[stage, o],
                device_id=back[o], device_id_type=MESH)
            for o in (2, 3, 0, 1)
        ]

    def coarse_copies(stage):
        return [
            pltpu.make_async_remote_copy(
                src_ref=csend.at[stage, o], dst_ref=crecv.at[stage, o],
                send_sem=cs_sem.at[stage, o], recv_sem=cr_sem.at[stage, o],
                device_id=ahead[o], device_id_type=MESH)
            for o in (2, 3, 0, 1)
        ]

    pl.semaphore_wait(barrier, len(greeted))
    for copy in round_1:
        copy.start()

    def z_traces(read, stage):
        for v in range(NVAR):
            zsend[stage, 0, v] = read(v, pl.ds(7, FACE, stride=8))
            zsend[stage, 1, v] = read(v, pl.ds(0, FACE, stride=8))

    def read_state(v, rows):
        return u[v, rows, :]

    def read_rate(v, rows):
        values = rate_1[v, rows, :]
        return jnp.broadcast_to(negative[0:1], values.shape) * values

    def row_of(first):
        parts = [ints_ref[first + o : first + o + 1, 0:CAP] for o in range(OFFS)]
        return eight(jnp.concatenate(parts, axis=1))

    def live_of(row):
        count = jnp.broadcast_to(ints_ref[row : row + 1, 0:1], (8, LANES))
        for o in range(1, OFFS):
            count = jnp.where(block == o, jnp.broadcast_to(ints_ref[row : row + 1, o : o + 1], (8, LANES)), count)
        return lane % CAP < count

    neighbour = eight(ints_ref[8:9])
    coarse_index = row_of(16)
    quadrant = row_of(24)
    fine_index = row_of(32)
    turns = row_of(40)
    coarse_live = live_of(48)
    fine_live = live_of(56)
    own_a = quadrant >= 2
    own_c = quadrant % 2 == 1
    back_turns = (4 - turns) % 4
    group_pick = block * CAP + (lane % 8) * 4
    group_index = lane_pick(coarse_index, group_pick)
    group_block = (lane // 8) % 4
    widen = [block * CAP + k * 8 + (lane % CAP) // 4 for k in range(4)]

    def rev(x):
        return jnp.take_along_axis(x, flipped, axis=0, mode="promise_in_bounds")

    def rotated(read, amount):
        odd = amount % 2 == 1
        far = amount >= 2
        mixed = [
            jnp.where(odd, read(pl.ds(7 - i, 8, stride=8)), read(pl.ds(8 * i, 8)))
            for i in range(8)
        ]
        return [jnp.where(far, rev(mixed[7 - i]), mixed[i]) for i in range(8)]

    def half_both(matrix, upper_a, upper_c, values, v):
        along_a = half_map(matrix, upper_a, values)
        for i in range(8):
            work[v, pl.ds(8 * i, 8), :] = along_a[i]
        columns = [work[v, pl.ds(j, 8, stride=8), :] for j in range(8)]
        return half_map(matrix, upper_c, columns)

    def send_mortars(read, stage, fine, coarse):
        def fine_side(v):
            for a in range(8):
                work[v, pl.ds(8 * a, 8), :] = lane_pick(read(v, pl.ds(64 * a, 8)), fine_index)
            turned = rotated(lambda rows: work[v, rows, :], back_turns)
            for a in range(8):
                own_fine[stage, v, pl.ds(8 * a, 8), :] = turned[a]
            for h in range(2):
                blocks = swap_blocks(turned[4 * h : 4 * h + 4], lane)
                for o in range(OFFS):
                    fsend[stage, o, tile(2 * v + h), :] = blocks[o]

        loop(NVAR, fine_side, UNROLL_SEND)
        for copy in fine:
            copy.start()

        def coarse_side(v):
            for h in range(2):
                pack = lane_pick(read(v, pl.ds(256 * h + 56, 8)), group_index)
                for k in range(1, 4):
                    top = read(v, pl.ds(256 * h + 64 * k + 56, 8))
                    pack = jnp.where(group_block == k, lane_pick(top, group_index), pack)
                packed[2 * v + h] = pack

        loop(NVAR, coarse_side, UNROLL_SEND)
        packed[10] = quadrant.astype(jnp.float32)
        packed[11] = jnp.zeros((8, LANES), jnp.float32)
        for m in range(3):
            blocks = swap_blocks([packed[4 * m + k] for k in range(4)], lane)
            for o in range(OFFS):
                csend[stage, o, pl.ds(8 * m, 8), :] = blocks[o]
        for copy in coarse:
            copy.start()

    def own_interpolated(read, stage):
        def one(v):
            picked = [lane_pick(read(v, pl.ds(64 * a + 56, 8)), coarse_index) for a in range(8)]
            columns = half_both(HALF, own_a, own_c, picked, v)
            for j in range(8):
                own_coarse[stage, v, pl.ds(j, 8, stride=8), :] = columns[j]

        loop(NVAR, one, UNROLL_OWN)

    total_rate = [rate_1]

    def line(read, normal, pressure, direction, v):
        if v == 0:
            return [read(1 + direction, j) for j in range(8)]
        if v == 4:
            return [normal[j] * (read(4, j) + pressure[j]) for j in range(8)]
        if v == 1 + direction:
            return [read(v, j) * normal[j] + pressure[j] for j in range(8)]
        return [read(v, j) * normal[j] for j in range(8)]

    def volume(state, direction, at, fresh):
        first = state is u

        def one(i):
            normal = [prim[direction, at(i, j), :] for j in range(8)]
            pressure = [prim[3, at(i, j), :] for j in range(8)]
            for v in range(0 if first else 1, NVAR):
                out = derive(line(lambda w, j: state[w, at(i, j), :], normal, pressure, direction, v))
                for j in range(8):
                    total = out[j] if fresh else total_rate[0][v, at(i, j), :] + out[j]
                    total_rate[0][v, at(i, j), :] = total
                    if v == 0 and direction == 0:
                        density_1[at(i, j), :] = total

        loop(8, one, UNROLL_VOLUME)

    def density_of_rate(direction, at, fresh):
        def one(i):
            out = derive([rate_1[1 + direction, at(i, j), :] for j in range(8)])
            for j in range(8):
                if fresh:
                    density_2[at(i, j), :] = out[j]
                else:
                    density_2[at(i, j), :] += out[j]

        loop(8, one, UNROLL_VOLUME)

    def lines_z(a, j):
        return pl.ds(a * 64 + j, 8, stride=8)

    def lines_y(a, j):
        return pl.ds(pl.multiple_of(a * 64 + j * 8, 8), 8)

    def lines_x(b, j):
        return pl.ds(pl.multiple_of(b * 8 + j * 64, 8), 8)

    def volume_z(state):
        volume(state, 2, lines_z, True)

    def volume_y(state):
        volume(state, 1, lines_y, False)

    def volume_x(state):
        volume(state, 0, lines_x, False)

    def inverse_of(row, counts):
        table = jnp.where(spread == row, 1.0, 0.0).astype(jnp.bfloat16)
        found = lax.dot_general(
            counts.astype(jnp.bfloat16), table, (((1,), (1,)), ((), ())),
            preferred_element_type=jnp.float32,
        )
        present = found > 0.5
        return jnp.maximum(found - 1.0, 0.0).astype(jnp.int32), present

    x_source, _ = inverse_of(neighbour[0:1], counting)
    c_source, c_present = inverse_of(coarse_index[0:1], jnp.where(lane % 4 == 0, counting, 0.0))
    f_source, f_present = inverse_of(fine_index[0:1], counting)

    def x_faces(state):
        def one(i):
            low = pl.ds(pl.multiple_of(i * 16, 16), 16)
            high = pl.ds(pl.multiple_of(448 + i * 16, 16), 16)
            pick = jnp.broadcast_to(neighbour[0:1], (16, LANES))
            source = jnp.broadcast_to(x_source[0:1], (16, LANES))
            left = [state[v, high, :] for v in range(NVAR)]
            right = [lane_pick(state[v, low, :], pick) for v in range(NVAR)]
            mean, jump = face_parts(left, right, 0)
            for v in range(NVAR):
                total_rate[0][v, high, :] += LIFT * (mean[v] - jump[v])
                total_rate[0][v, low, :] += LIFT * lane_pick(mean[v] + jump[v], source)

        loop(4, one, UNROLL_FACE)

    def blend(ref, index, factor):
        if factor is None:
            return ref[(0,) + index]
        first = ref[(0,) + index]
        return first + jnp.broadcast_to(factor, first.shape) * ref[(1,) + index]

    def z_faces(factor):
        def one(i):
            rows = pl.ds(pl.multiple_of(i * 16, 16), 16)
            bottom = pl.ds(i * 128, 16, stride=8)
            top = pl.ds(i * 128 + 7, 16, stride=8)
            left = [blend(zsend, (0, v, rows, slice(None)), factor) for v in range(NVAR)]
            right = [blend(zrecv, (1, v, rows, slice(None)), factor) for v in range(NVAR)]
            mean, jump = face_parts(left, right, 2)
            for v in range(NVAR):
                total_rate[0][v, top, :] += LIFT * (mean[v] - jump[v])
            left = [blend(zrecv, (0, v, rows, slice(None)), factor) for v in range(NVAR)]
            right = [blend(zsend, (1, v, rows, slice(None)), factor) for v in range(NVAR)]
            mean, jump = face_parts(left, right, 2)
            for v in range(NVAR):
                total_rate[0][v, bottom, :] += LIFT * (mean[v] + jump[v])

        loop(4, one, UNROLL_FACE)

    def far_quadrants():
        far = packed[10]
        return far > 1.5, (far == 1.0) | (far == 3.0)

    def expand(stage):
        for m in range(3):
            blocks = swap_blocks([crecv[stage, o, pl.ds(8 * m, 8), :] for o in range(OFFS)], lane)
            for k in range(4):
                packed[4 * m + k] = blocks[k]
        far_a, far_c = far_quadrants()

        def one(v):
            for h in range(2):
                blocks = swap_blocks([frecv[stage, o, tile(2 * v + h), :] for o in range(OFFS)], lane)
                for k in range(4):
                    far_fine[stage, v, pl.ds(8 * (4 * h + k), 8), :] = blocks[k]
            picked = [lane_pick(packed[2 * v + a // 4], widen[a % 4]) for a in range(8)]
            columns = half_both(HALF, far_a, far_c, picked, v)
            for j in range(8):
                far_coarse[stage, v, pl.ds(j, 8, stride=8), :] = columns[j]

        loop(NVAR, one, UNROLL_EXPAND)

    def mortar_terms(factor):
        def fluxes(i):
            rows = pl.ds(pl.multiple_of(i * 16, 16), 16)
            live = jnp.concatenate([coarse_live, coarse_live], axis=0)
            left = [blend(own_coarse, (v, rows, slice(None)), factor) for v in range(NVAR)]
            right = [blend(far_fine, (v, rows, slice(None)), factor) for v in range(NVAR)]
            mean, jump = face_parts(left, right, 1)
            for v in range(NVAR):
                coarse_term[v, rows, :] = jnp.where(live, mean[v] - jump[v], 0.0)
            live = jnp.concatenate([fine_live, fine_live], axis=0)
            left = [blend(far_coarse, (v, rows, slice(None)), factor) for v in range(NVAR)]
            right = [blend(own_fine, (v, rows, slice(None)), factor) for v in range(NVAR)]
            mean, jump = face_parts(left, right, 1)
            for v in range(NVAR):
                fine_term[v, rows, :] = jnp.where(live, mean[v] + jump[v], 0.0)

        loop(4, fluxes, UNROLL_FACE)

        def scatter(v):
            values = [coarse_term[v, pl.ds(8 * a, 8), :] for a in range(8)]
            columns = half_both(BACK, own_a, own_c, values, v)
            for c in range(8):
                total = columns[c] + pltpu.roll(columns[c], 127, 1)
                total = total + pltpu.roll(total, 126, 1)
                share = jnp.where(c_present, lane_pick(total, c_source), 0.0)
                total_rate[0][v, pl.ds(56 + c, 8, stride=64), :] += LIFT * share
            turned = rotated(lambda rows: fine_term[v, rows, :], turns)
            for a in range(8):
                share = jnp.where(f_present, lane_pick(turned[a], f_source), 0.0)
                total_rate[0][v, pl.ds(64 * a, 8), :] += LIFT * share

        loop(NVAR, scatter, UNROLL_SCATTER)

    fine_first = fine_copies(0)
    coarse_first = coarse_copies(0)
    send_mortars(read_state, 0, fine_first, coarse_first)
    z_first = z_copies(0)
    z_traces(read_state, 0)
    for copy in z_first:
        copy.start()
    volume_z(u)
    volume_y(u)
    speed = finish_round(round_1, speed, 0)
    vsend[1, 0:1] = speed
    for copy in round_2:
        copy.start()
    volume_x(u)
    x_faces(u)
    own_interpolated(read_state, 0)
    speed = finish_round(round_2, speed, cuts - 1)
    vsend[2, 0:1] = speed
    for copy in round_3:
        copy.start()
    for copy in fine_first + coarse_first:
        copy.wait_recv()
    expand(0)
    mortar_terms(None)
    for copy in z_first:
        copy.wait_recv()
    z_faces(None)

    fine_second = fine_copies(1)
    coarse_second = coarse_copies(1)
    send_mortars(read_rate, 1, fine_second, coarse_second)
    z_second = z_copies(1)
    z_traces(read_rate, 1)
    for copy in z_second:
        copy.start()
    own_interpolated(read_rate, 1)
    density_of_rate(2, lines_z, True)
    density_of_rate(1, lines_y, False)
    density_of_rate(0, lines_x, False)
    speed = finish_round(round_3, speed, cuts + ys - 2)
    step = 0.005 / jnp.max(speed, axis=1, keepdims=True)
    scale = jnp.broadcast_to(negative[0:1] * step, (32, LANES))
    factor = section_b[0] * step
    scale_ref[...] = scale[0:8]
    blended = section_b[0] * scale

    def first_update(i):
        rows = pl.ds(pl.multiple_of(i * 32, 32), 32)
        state = []
        for v in range(NVAR):
            state.append(u[v, rows, :] + blended * rate_1[v, rows, :])
            sect[v, rows, :] = state[v]
        rate_2[0, rows, :] = density_1[rows, :] + blended * density_2[rows, :]
        inverse, velocity, pressure = primitives(state)
        for d in range(3):
            prim[d, rows, :] = velocity[d]
        prim[3, rows, :] = pressure

    loop(16, first_update, UNROLL_UPDATE)

    total_rate[0] = rate_2
    volume_z(sect)
    volume_y(sect)
    volume_x(sect)
    x_faces(sect)
    for copy in fine_second + coarse_second:
        copy.wait_recv()
    expand(1)
    mortar_terms(factor)
    for copy in z_second:
        copy.wait_recv()
    z_faces(factor)

    for copies in (round_1, round_2, round_3, z_first, z_second, fine_first, fine_second, coarse_first, coarse_second):
        for copy in copies:
            copy.wait_send()


def on_device(
    slabs, cuts, ys, zs,
    conserved,
    refinement,
    x_neighbour,
    coarse_element,
    quadrant,
    send_count,
    fine_element,
    orientation,
    receive_count,
):
    peers = cuts + ys + zs - 3
    state = (NVAR, NP * FACE, LANES)
    face = (NVAR, FACE, LANES)
    links = (OFFS, CAP)
    tables = (
        refinement.reshape(1, LANES), x_neighbour, coarse_element.reshape(links),
        quadrant.reshape(links), fine_element.reshape(links), orientation.reshape(links),
        send_count.reshape(1, OFFS), receive_count.reshape(1, OFFS),
    )
    ints = jnp.zeros((64, LANES), jnp.int32)
    for i, table in enumerate(tables):
        rows, columns = table.shape
        ints = jnp.maximum(ints, jnp.pad(table, ((8 * i, 64 - 8 * i - rows), (0, LANES - columns))))
    rate_1, rate_2, sectioned, scale = pl.pallas_call(
        functools.partial(kernel, slabs, cuts, ys, zs),
        out_shape=[jax.ShapeDtypeStruct(state, jnp.float32)] * 3
        + [jax.ShapeDtypeStruct((8, LANES), jnp.float32)],
        in_specs=[pl.BlockSpec(memory_space=pltpu.HBM), pl.BlockSpec(memory_space=pltpu.VMEM)],
        out_specs=[pl.BlockSpec(memory_space=pltpu.VMEM)] * 4,
        scratch_shapes=[
            pltpu.VMEM(state, jnp.float32),
            pltpu.VMEM((4, NP * FACE, LANES), jnp.float32),
            pltpu.VMEM((NP * FACE, LANES), jnp.float32),
            pltpu.VMEM((NP * FACE, LANES), jnp.float32),
            pltpu.VMEM((2, 2) + face, jnp.float32),
            pltpu.VMEM((2, 2) + face, jnp.float32),
            pltpu.VMEM((2, OFFS, 24, LANES), jnp.float32),
            pltpu.VMEM((2, OFFS, 24, LANES), jnp.float32),
            pltpu.VMEM((2, OFFS, 80, LANES), jnp.float32),
            pltpu.VMEM((2, OFFS, 80, LANES), jnp.float32),
            pltpu.VMEM((3, 8, LANES), jnp.float32),
            pltpu.VMEM((peers, 8, LANES), jnp.float32),
            pltpu.VMEM((2,) + face, jnp.float32),
            pltpu.VMEM((2,) + face, jnp.float32),
            pltpu.VMEM((2,) + face, jnp.float32),
            pltpu.VMEM((2,) + face, jnp.float32),
            pltpu.VMEM(face, jnp.float32),
            pltpu.VMEM(face, jnp.float32),
            pltpu.VMEM(face, jnp.float32),
            pltpu.VMEM((12, 8, LANES), jnp.float32),
            pltpu.SemaphoreType.DMA((8,)),
            pltpu.SemaphoreType.DMA((2, 2)),
            pltpu.SemaphoreType.DMA((2, 2)),
            pltpu.SemaphoreType.DMA((2, OFFS)),
            pltpu.SemaphoreType.DMA((2, OFFS)),
            pltpu.SemaphoreType.DMA((2, OFFS)),
            pltpu.SemaphoreType.DMA((2, OFFS)),
            pltpu.SemaphoreType.DMA((peers,)),
            pltpu.SemaphoreType.DMA((peers,)),
        ],
        compiler_params=pltpu.CompilerParams(
            collective_id=0, has_side_effects=True, vmem_limit_bytes=50 * 1024 * 1024
        ),
    )(conserved, ints)
    register = scale[0] * (section_a[1] * rate_1 + rate_2)
    return sectioned + section_b[1] * register, register


def solution(mesh):
    slabs, cuts = mesh.shape["slab"], mesh.shape["cut"]
    zs = 12 if slabs % 12 == 0 else 3
    return jax.shard_map(
        functools.partial(on_device, slabs, cuts, slabs // zs, zs),
        mesh=mesh,
        in_specs=(
            P(None, None, ("slab", "cut")),
            P(("slab", "cut")),
            P(("slab", "cut"), None),
            P("slab", "cut", None, None),
            P("slab", "cut", None, None),
            P("slab", "cut", None),
            P("slab", "cut", None, None),
            P("slab", "cut", None, None),
            P("slab", "cut", None),
        ),
        out_specs=(P(None, None, ("slab", "cut")), P(None, None, ("slab", "cut"))),
        check_vma=False,
    )
```
